32 devices in a mesh: ctx: 16 (over z, y, x), tp: 2 (over core).
Axes of the slice: x: 2, y: 2, z: 4, core: 2. Of those that a mesh axis runs over, the one named last changes fastest.
Arguments:
- queries: bfloat16 [4096, 8192], P('ctx', 'tp'), may hold values from -128 to 128
- cotangent: bfloat16 [4096, 8192], P('ctx', 'tp'), may hold values from -96 to 96
- image_keys: bfloat16 [16, 64, 1024], P('ctx', None, 'tp'), may hold values from -8 to 8
- image_values: bfloat16 [16, 64, 1024], P('ctx', None, 'tp'), may hold values from -6 to 6
- attn_gate: float32 [1], replicated, may hold values from 0.4 to 1.5
- block_mask: int32 [32, 16], P('ctx'), may hold values from 0 to 1, as said below
- image_owner: int32 [16], replicated, may hold values from 0 to 15, each once
Outputs:
- query_grad: bfloat16 [4096, 8192], P('ctx', 'tp')
- key_grad: bfloat16 [16, 64, 1024], P('ctx', None, 'tp')
- value_grad: bfloat16 [16, 64, 1024], P('ctx', None, 'tp')
- gate_grad: float32 [1], replicated
The draws below stay inside these ranges and needn't reach their ends.
Inputs may be any that keep to these rules, and one draw needn't show every extreme that they name: `block_mask`: every text block reads at least one image; the 2 blocks of one index of ctx together read exactly 8 distinct images.
All inputs are finite; a program needn't handle non-finite values.
Results may differ from the reference program's by a relative error of at most 0.02.
Values may be sent and summed in bfloat16 or wider, within the bound.
No kernel may reach another device: no remote copies, remote signals or barrier semaphores. Data moves between devices by JAX's collectives and lax.ppermute only.
A program may use at most 64 MiB of HBM per device.

```python
import math
import jax
import jax.numpy as jnp
from jax import lax

H = 64
KVH = 8
HD = 128
TOK_DEV = 256
BLK = 128
IMG_TOK = 64
NIMG = 16
RMAX = 8
TEXT = 4096
NBLK = 32
BLK_DEV = 2
N_CTX = 16


def draw_queries(key, part):
    entries = jax.random.normal(jax.random.fold_in(key, 1), (TEXT, H * HD), jnp.float32)
    return entries.astype(jnp.bfloat16)


def draw_image_keys(key, part):
    entries = jax.random.normal(jax.random.fold_in(key, 3), (NIMG, IMG_TOK, KVH * HD), jnp.float32)
    return entries.astype(jnp.bfloat16)


def draw_block_mask(key, part):
    shards = NBLK // BLK_DEV
    key_perm, key_bits = jax.random.split(key, 2)
    orders = jax.vmap(lambda subkey: jax.random.permutation(subkey, NIMG))(jax.random.split(key_perm, shards))
    positions = jnp.argsort(orders, axis=1)
    coin_flips = jax.random.randint(key_bits, (shards, BLK_DEV, NIMG), 0, 2)
    block_index = jnp.arange(BLK_DEV)[None, :, None]
    position_grid = positions[:, None, :]
    chosen = position_grid < RMAX
    reading = chosen & ((position_grid % BLK_DEV == block_index) | (position_grid == 0) | (coin_flips == 1))
    return reading.astype(jnp.int32).reshape(NBLK, NIMG)


def steps_of(stream_key, extent, pieces, least, top_value):
    level, own = 1.0, jax.random.fold_in(stream_key, 6)
    for position, shards_of in pieces:
        draws = jnp.exp(jax.random.uniform(jax.random.fold_in(own, position), (shards_of,), jnp.float32, least / len(pieces), top_value / len(pieces)))
        level = level * jnp.repeat(draws, extent[position] // shards_of).reshape([-1 if axis == position else 1 for axis in range(len(extent))])
    return level


def noise(stream_key, shape, spread, reach, cuts=(), kind=jnp.bfloat16):
    factor_of = steps_of(stream_key, shape, cuts, -0.22, 0.18) if cuts else 1.0
    result = jax.random.normal(stream_key, shape, jnp.float32) * spread * factor_of
    return jnp.minimum(jnp.maximum(result, -reach), reach).astype(kind)


def setup_inputs(seed: int = 0) -> dict:
    streams_of = jax.random.split(jax.random.key(seed), 8)
    queries = draw_queries(jax.random.fold_in(streams_of[7], 71), 0)
    cotangent = noise(streams_of[1], (TEXT, H * HD), 16.0, 96.0, ((0, 16), (1, 2)))
    image_keys = draw_image_keys(jax.random.fold_in(streams_of[7], 71), 0)
    image_values = noise(streams_of[3], (NIMG, IMG_TOK, KVH * HD), 1.0, 6.0, ((0, 16), (2, 2)))
    attn_gate = jnp.clip(jax.random.uniform(streams_of[4], (1,), jnp.float32, 0.4, 1.5), 0.4, 1.5)
    block_mask = draw_block_mask(jax.random.fold_in(streams_of[7], 71), 0)
    image_owner = jax.random.permutation(streams_of[6], NIMG).astype(jnp.int32)
    return dict(queries=queries, cotangent=cotangent, image_keys=image_keys, image_values=image_values, attn_gate=attn_gate, block_mask=block_mask, image_owner=image_owner)


def select_images(mask_rows, image_owner):
    read_any = lax.optimization_barrier(jnp.max(mask_rows, axis=0))
    ranking = read_any * (2 * NIMG) + (NIMG - 1 - jnp.arange(NIMG, dtype=jnp.int32))
    top_vals, image_ids = lax.top_k(ranking, RMAX)
    image_ids = image_ids.astype(jnp.int32)
    is_read = read_any[image_ids] > 0
    slot_ids = image_owner[image_ids].astype(jnp.int32)
    block_keep = (mask_rows[:, image_ids] > 0) & is_read[None, :]
    keep_mask = jnp.repeat(jnp.repeat(block_keep, BLK, axis=0), IMG_TOK, axis=1)
    return (slot_ids, is_read, keep_mask)

def group_backward(query_rows, cot_rows, key_rows, value_rows, keep_mask, gate_value):
    groups = H // KVH
    inv_root = 1.0 / math.sqrt(HD)
    query_f = query_rows.reshape(TOK_DEV, KVH, groups, HD).astype(jnp.float32)
    key_f = key_rows.reshape(RMAX * IMG_TOK, KVH, HD).astype(jnp.float32)
    value_f = value_rows.reshape(RMAX * IMG_TOK, KVH, HD).astype(jnp.float32)
    scores = jnp.einsum('tkgd,skd->kgts', query_f, key_f) * inv_root
    scores = jnp.where(keep_mask, scores, -1e+30)
    row_max = lax.optimization_barrier(jnp.max(scores, axis=-1, keepdims=True))
    exp_terms = jnp.where(keep_mask, jnp.exp(scores - row_max), 0.0)
    prob_full = exp_terms / lax.optimization_barrier(jnp.sum(exp_terms, axis=-1, keepdims=True))
    prob_half = prob_full.astype(jnp.bfloat16)
    attended = jnp.einsum('kgts,skd->tkgd', prob_half.astype(jnp.float32), value_f)
    cot_f = cot_rows.reshape(TOK_DEV, KVH, groups, HD).astype(jnp.float32)
    gate_part = jnp.sum(cot_f * attended)
    attn_grad = (gate_value * cot_f).astype(jnp.bfloat16)
    grad_f = attn_grad.astype(jnp.float32)
    prob_grad = jnp.einsum('tkgd,skd->kgts', grad_f, value_f)
    row_delta = jnp.einsum('tkgd,tkgd->kgt', grad_f, attended)
    score_grad = (prob_full * (prob_grad - row_delta[..., None]) * inv_root).astype(jnp.bfloat16)
    score_f = score_grad.astype(jnp.float32)
    query_grad = jnp.einsum('kgts,skd->tkgd', score_f, key_f).astype(jnp.bfloat16)
    key_grad = jnp.einsum('kgts,tkgd->skd', score_f, query_f)
    value_grad = jnp.einsum('kgts,tkgd->skd', prob_half.astype(jnp.float32), grad_f)
    return (query_grad.reshape(TOK_DEV, H * HD), key_grad, value_grad, gate_part)

def reference(queries, cotangent, image_keys, image_values, attn_gate, block_mask, image_owner):
    gate_value = jnp.tanh(attn_gate[0])
    query_groups = queries.reshape(N_CTX, TOK_DEV, H * HD)
    cot_groups = cotangent.reshape(N_CTX, TOK_DEV, H * HD)
    mask_groups = block_mask.reshape(N_CTX, BLK_DEV, NIMG)

    def group_step(state_in, group_inputs):
        grads_acc, gate_acc = state_in
        query_rows, cot_rows, mask_rows = group_inputs
        slot_ids, is_read, keep_mask = select_images(mask_rows, image_owner)
        key_rows = image_keys[slot_ids]
        value_rows = image_values[slot_ids]
        query_grad, key_grad, value_grad, gate_part = group_backward(query_rows, cot_rows, key_rows, value_rows, keep_mask, gate_value)
        stacked = jnp.concatenate([key_grad.reshape(RMAX, IMG_TOK, KVH * HD), value_grad.reshape(RMAX, IMG_TOK, KVH * HD)], axis=-1)
        stacked = jnp.where(is_read[:, None, None], stacked, 0.0)
        grads_acc = grads_acc.at[slot_ids].add(stacked)
        return ((grads_acc, gate_acc + gate_part), query_grad)
    init_state = (jnp.zeros((NIMG, IMG_TOK, 2 * KVH * HD), jnp.float32), jnp.zeros((), jnp.float32))
    (grads_acc, gate_acc), query_all = lax.scan(group_step, init_state, (query_groups, cot_groups, mask_groups))
    key_grad = grads_acc[:, :, :KVH * HD].astype(jnp.bfloat16)
    value_grad = grads_acc[:, :, KVH * HD:].astype(jnp.bfloat16)
    gate_grad = ((1.0 - gate_value * gate_value) * gate_acc / math.sqrt(TEXT * H * HD)).reshape(1).astype(jnp.float32)
    return (query_all.reshape(TEXT, H * HD), key_grad, value_grad, gate_grad)
```

```python
import functools
import math

import jax
import jax.numpy as jnp
from jax import lax
from jax.experimental import pallas as pl
from jax.experimental.pallas import tpu as pltpu
from jax.sharding import PartitionSpec as P

HD = 128
BLK = 128
PAIR = 2
CHUNKS = 2
NT = (((1,), (1,)), ((), ()))


def attention_kernel(
    n_outer,
    has_prev,
    mask_ref,
    owner_ref,
    me_ref,
    gate_ref,
    q_ref,
    cot_ref,
    k_own,
    k_x,
    k_yd,
    v_own,
    v_y,
    v_xd,
    *rest,
):
    if has_prev:
        rest = rest[1:]
    (
        dq_ref,
        dk_own,
        dk_x,
        dk_yd,
        dv_own,
        dv_y,
        dv_xd,
        gate_out,
        k_all,
        v_all,
        k_sel,
        v_sel,
        kt_sel,
        dk_acc,
        dv_acc,
        dk_all,
        dv_all,
        gate_acc,
        place,
        bias,
    ) = rest
    n_blocks, n_images = mask_ref.shape
    img_tok = k_own.shape[1]
    read_most = n_images // 2
    groups = q_ref.shape[1] // HD
    step = pl.program_id(0)
    gate_value = gate_ref[0]
    inv_root = 1.0 / math.sqrt(HD)
    to_exp2 = math.log2(math.e) * inv_root

    @pl.when(step == 0)
    def _():
        gate_acc[...] = jnp.zeros_like(gate_acc)
        me = me_ref[0]
        for j in range(read_most):
            place[j] = 0
            for b in range(n_blocks):
                bias[b, j] = jnp.float32(-1e30)

        def look(i, count):
            reads = [mask_ref[b, i] > 0 for b in range(n_blocks)]
            any_read = functools.reduce(jnp.logical_or, reads)

            @pl.when(jnp.logical_and(any_read, count < read_most))
            def _():
                slot = owner_ref[i]
                column = jnp.bitwise_xor(lax.rem(slot, 4), lax.rem(me, 4))
                back = lax.rem(lax.div(me, 4) - lax.div(slot, 4) + n_outer, n_outer)
                place[count] = column * n_outer + back
                for b in range(n_blocks):
                    bias[b, count] = jnp.where(reads[b], 0.0, -1e30).astype(jnp.float32)

            return count + any_read.astype(jnp.int32)

        lax.fori_loop(0, n_images, look, jnp.int32(0))

    n = n_outer
    k_all[0:n] = k_own[...]
    k_all[n : 2 * n] = k_x[...]
    k_all[2 * n : 4 * n] = k_yd[...]
    v_all[0:n] = v_own[...]
    v_all[n : 2 * n] = v_xd[0:n]
    v_all[2 * n : 3 * n] = v_y[...]
    v_all[3 * n : 4 * n] = v_xd[n : 2 * n]
    for j in range(read_most):
        rows = slice(j * img_tok, (j + 1) * img_tok)
        k_sel[rows] = k_all[place[j]]
        v_sel[rows] = v_all[place[j]]
    kt_sel[...] = k_sel[...].astype(jnp.float32).T.astype(jnp.bfloat16)
    dk_acc[...] = jnp.zeros_like(dk_acc)
    dv_acc[...] = jnp.zeros_like(dv_acc)

    pairs = groups // PAIR

    def one(it, carry):
        b = it // pairs
        g = it % pairs
        rows = pl.ds(pl.multiple_of(b * BLK, BLK), BLK)

        def heads_of(ref):
            return jnp.concatenate(
                [
                    ref[rows, pl.ds(pl.multiple_of((g * PAIR + u) * HD, HD), HD)]
                    for u in range(PAIR)
                ],
                axis=0,
            )

        query = heads_of(q_ref)
        cot = heads_of(cot_ref)
        scores = lax.dot_general(k_sel[...], query, NT, preferred_element_type=jnp.float32)
        scores = jnp.concatenate(
            [scores[j * img_tok : (j + 1) * img_tok] + bias[b, j] for j in range(read_most)],
            axis=0,
        )
        row_max = jnp.max(scores, axis=0, keepdims=True)
        terms = jnp.exp2((scores - row_max) * to_exp2)
        prob = terms * (1.0 / jnp.sum(terms, axis=0, keepdims=True))
        prob_half = prob.astype(jnp.bfloat16)
        prob_grad = lax.dot_general(v_sel[...], cot, NT, preferred_element_type=jnp.float32)
        delta = jnp.sum(prob_half.astype(jnp.float32) * prob_grad, axis=0, keepdims=True)
        score_grad = (prob * (prob_grad - delta)).astype(jnp.bfloat16)
        dq_t = jnp.dot(kt_sel[...], score_grad, preferred_element_type=jnp.float32)
        dq = (dq_t.T * (gate_value * inv_root)).astype(jnp.bfloat16)
        for u in range(PAIR):
            lanes = pl.ds(pl.multiple_of((g * PAIR + u) * HD, HD), HD)
            dq_ref[rows, lanes] = dq[u * BLK : (u + 1) * BLK]
        dk_acc[...] += jnp.dot(score_grad, query, preferred_element_type=jnp.float32)
        dv_acc[...] += jnp.dot(prob_half, cot, preferred_element_type=jnp.float32)
        gate_acc[0:1, :] += delta
        return carry

    lax.fori_loop(0, n_blocks * pairs, one, 0)

    dk_all[...] = jnp.zeros_like(dk_all)
    dv_all[...] = jnp.zeros_like(dv_all)
    for j in range(read_most):
        rows = slice(j * img_tok, (j + 1) * img_tok)
        dk_all[place[j]] = dk_acc[rows] * (gate_value * inv_root)
        dv_all[place[j]] = dv_acc[rows] * gate_value
    dk_own[...] = dk_all[0:n]
    dk_x[...] = dk_all[n : 2 * n]
    dk_yd[...] = dk_all[2 * n : 4 * n].astype(jnp.bfloat16)
    dv_own[...] = dv_all[0:n]
    dv_xd[0:n] = dv_all[n : 2 * n].astype(jnp.bfloat16)
    dv_y[...] = dv_all[2 * n : 3 * n]
    dv_xd[n : 2 * n] = dv_all[3 * n : 4 * n].astype(jnp.bfloat16)

    @pl.when(step == pl.num_programs(0) - 1)
    def _():
        gate_out[...] = jnp.full(gate_out.shape, jnp.sum(gate_acc[...]), jnp.float32)


def attention(first, heads, n_outer, prev, scalars, queries, cotangent, keys, values):
    tokens = queries.shape[0]
    local_kv = keys[0].shape[2] // HD * (1 if heads is None else 1)
    img_tok = keys[0].shape[1]
    n_images = scalars[0].shape[1]
    total_kv = scalars[4]
    groups = queries.shape[1] // HD // total_kv
    width = groups * HD
    n_keys = n_images // 2 * img_tok
    n = n_outer
    smem = pl.BlockSpec(memory_space=pltpu.SMEM)
    wide = pl.BlockSpec((tokens, width), lambda i: (0, first + i))

    def cols(count):
        return pl.BlockSpec((count, img_tok, HD), lambda i: (0, 0, i))

    in_specs = [smem] * 4 + [wide, wide]
    in_specs += [cols(n), cols(n), cols(2 * n)] * 2
    args = [*scalars[:4], queries, cotangent, *keys, *values]
    aliases = {}
    if prev is not None:
        in_specs.append(pl.BlockSpec(memory_space=pl.ANY))
        aliases = {len(args): 0}
        args.append(prev)
    span = heads * HD
    f32, bf16 = jnp.float32, jnp.bfloat16
    out_shape = [jax.ShapeDtypeStruct(queries.shape, bf16)]
    for _ in range(2):
        out_shape += [
            jax.ShapeDtypeStruct((n, img_tok, span), f32),
            jax.ShapeDtypeStruct((n, img_tok, span), f32),
            jax.ShapeDtypeStruct((2 * n, img_tok, span), bf16),
        ]
    out_shape.append(jax.ShapeDtypeStruct((8, HD), f32))
    out_specs = [wide] + [cols(n), cols(n), cols(2 * n)] * 2
    out_specs.append(pl.BlockSpec((8, HD), lambda i: (0, 0)))
    rows = tokens * groups * heads
    return pl.pallas_call(
        functools.partial(attention_kernel, n, prev is not None),
        grid=(heads,),
        in_specs=in_specs,
        out_specs=out_specs,
        out_shape=out_shape,
        input_output_aliases=aliases,
        scratch_shapes=[
            pltpu.VMEM((4 * n, img_tok, HD), bf16),
            pltpu.VMEM((4 * n, img_tok, HD), bf16),
            pltpu.VMEM((n_keys, HD), bf16),
            pltpu.VMEM((n_keys, HD), bf16),
            pltpu.VMEM((HD, n_keys), bf16),
            pltpu.VMEM((n_keys, HD), f32),
            pltpu.VMEM((n_keys, HD), f32),
            pltpu.VMEM((4 * n, img_tok, HD), f32),
            pltpu.VMEM((4 * n, img_tok, HD), f32),
            pltpu.VMEM((8, PAIR * BLK), f32),
            pltpu.SMEM((n_images // 2,), jnp.int32),
            pltpu.SMEM((scalars[0].shape[0], n_images // 2), f32),
        ],
        compiler_params=pltpu.CompilerParams(
            dimension_semantics=("arbitrary",), vmem_limit_bytes=48 * 1024 * 1024
        ),
        cost_estimate=pl.CostEstimate(
            flops=10 * rows * n_keys * HD,
            bytes_accessed=6 * rows * HD,
            transcendentals=rows * n_keys,
        ),
        name="attention_backward",
    )(*args)


def per_device(queries, cotangent, image_keys, image_values, attn_gate, block_mask, image_owner):
    n_ctx = lax.axis_size("ctx")
    n_tp = lax.axis_size("tp")
    n = n_ctx // 4
    local_kv = image_keys.shape[2] // HD
    chunks = min(CHUNKS, local_kv)
    heads = local_kv // chunks
    me = lax.axis_index("ctx").astype(jnp.int32).reshape(1)
    gate_value = jnp.tanh(attn_gate)
    f32, bf16 = jnp.float32, jnp.bfloat16

    def swap(value, bit):
        return lax.ppermute(value, "ctx", [(i, i ^ bit) for i in range(n_ctx)])

    def turn(value, by):
        pairs = [(i, (i // 4 + by) % n * 4 + i % 4) for i in range(n_ctx)]
        return lax.ppermute(value, "ctx", pairs)

    lanes = [slice(c * heads * HD, (c + 1) * heads * HD) for c in range(chunks)]
    columns = []
    for c in range(chunks):
        own = jnp.concatenate([image_keys[0, :, lanes[c]], image_values[0, :, lanes[c]]], axis=0)
        columns.append(jnp.stack([own] + [turn(own, k) for k in range(1, n)]))
    img_tok = image_keys.shape[1]
    gathered = []
    for c in range(chunks):
        k_own, v_own = columns[c][:, :img_tok], columns[c][:, img_tok:]
        k_x, v_y = swap(k_own, 1), swap(v_own, 2)
        k_yd = swap(jnp.concatenate([k_own, k_x]), 2)
        v_xd = swap(jnp.concatenate([v_own, v_y]), 1)
        gathered.append(((k_own, k_x, k_yd), (v_own, v_y, v_xd)))

    scalars = (block_mask, image_owner, me, gate_value, local_kv)
    dq = None
    key_parts, value_parts, gate_parts = [], [], []
    for c in range(chunks):
        keys, values = gathered[c]
        dq, dk_own, dk_x, dk_yd, dv_own, dv_y, dv_xd, gate_part = attention(
            c * heads, heads, n, dq, scalars, queries, cotangent, keys, values
        )
        gate_parts.append(gate_part)
        k_back, v_back = swap(dk_yd, 2), swap(dv_xd, 1)
        k_send = (dk_x + k_back[n:].astype(f32)).astype(bf16)
        v_send = (dv_y + v_back[n:].astype(f32)).astype(bf16)
        k_last, v_last = swap(k_send, 1), swap(v_send, 2)
        k_sum = dk_own + k_back[:n].astype(f32) + k_last.astype(f32)
        v_sum = dv_own + v_back[:n].astype(f32) + v_last.astype(f32)
        both = jnp.concatenate([k_sum, v_sum], axis=1)
        total = both[0]
        sends = both.astype(bf16)
        for k in range(1, n):
            total = total + turn(sends[k], -k).astype(f32)
        key_parts.append(total[:img_tok])
        value_parts.append(total[img_tok:])
    key_grad = jnp.concatenate(key_parts, axis=1).astype(bf16)[None]
    value_grad = jnp.concatenate(value_parts, axis=1).astype(bf16)[None]

    gate_sum = functools.reduce(jnp.add, gate_parts)

    def add_turns(value, axis, size, stride=1):
        total = value
        for k in range(1, size):
            pairs = [(i, (i + k) % size) for i in range(size)]
            total = total + lax.ppermute(value, axis, pairs)
        return total

    gate_sum = add_turns(gate_sum, "tp", n_tp)
    gate_sum = gate_sum + swap(gate_sum, 1)
    gate_sum = gate_sum + swap(gate_sum, 2)
    total = gate_sum
    for k in range(1, n):
        total = total + turn(gate_sum, k)
    term_count = queries.shape[0] * n_ctx * queries.shape[1] * n_tp
    gate_grad = (1.0 - gate_value * gate_value) * total[0, :1] / math.sqrt(term_count)
    return (dq, key_grad, value_grad, gate_grad)


def solution(mesh):
    in_specs = (
        P("ctx", "tp"),
        P("ctx", "tp"),
        P("ctx", None, "tp"),
        P("ctx", None, "tp"),
        P(),
        P("ctx", None),
        P(),
    )
    out_specs = (P("ctx", "tp"), P("ctx", None, "tp"), P("ctx", None, "tp"), P())
    return jax.shard_map(
        per_device, mesh=mesh, in_specs=in_specs, out_specs=out_specs, check_vma=False
    )
```

```python
import functools
import math

import jax
import jax.numpy as jnp
from jax import lax
from jax.experimental import pallas as pl
from jax.experimental.pallas import tpu as pltpu
from jax.sharding import PartitionSpec as P

HD = 128
BLK = 128
PAIR = 4
UNROLL = 2
CHUNKS = 2
CODE = 16
NT = (((1,), (1,)), ((), ()))
F32, BF16 = jnp.float32, jnp.bfloat16


def coded(value, rows, rounded):
    high = rounded(value)
    middle = rounded(value - high)
    low = value - high - middle
    shape = (rows, value.shape[1])
    row = lax.broadcasted_iota(jnp.int32, shape, 0)
    parts = jnp.where(row == 0, high, jnp.zeros(shape, F32))
    return jnp.where(row == 1, middle, jnp.where(row == 2, low, parts)).astype(BF16)


def rounded_here(value):
    return value.astype(BF16).astype(F32)


def rounded_outside(value):
    return lax.reduce_precision(value, 8, 7)


def decoded(rows):
    rows = rows.astype(F32)
    return rows[0:1] + rows[1:2] + rows[2:3]


def attention_kernel(n, two_step, n_extra, *refs):
    mask_ref, owner_ref, me_ref, gate_ref, gate_in, q_ref, cot_ref = refs[:7]
    k_cols, v_cols = refs[7:11], refs[11:15]
    refs = refs[15 + n_extra :]
    n_out = 6 if two_step else 5
    dq_ref, own_ref = refs[:2]
    back_refs = refs[2:n_out]
    (
        gate_out,
        k_all,
        v_all,
        k_sel,
        v_sel,
        kt_sel,
        dk_acc,
        dv_acc,
        dk_all,
        dv_all,
        gate_acc,
        place,
        bias,
    ) = refs[n_out:]
    n_blocks, n_images = mask_ref.shape
    img_tok = k_all.shape[1]
    read_most = n_images // 2
    groups = q_ref.shape[1] // HD
    step = pl.program_id(0)
    gate_value = gate_ref[0]
    inv_root = 1.0 / math.sqrt(HD)
    to_exp2 = math.log2(math.e) * inv_root

    @pl.when(step == 0)
    def _():
        gate_acc[...] = jnp.zeros_like(gate_acc)
        gate_acc[0:1, 0:HD] = gate_in[0:1, :]
        me = me_ref[0]
        for j in range(read_most):
            place[j] = 0
            for b in range(n_blocks):
                bias[b, j] = jnp.float32(-1e30)

        def look(i, count):
            reads = [mask_ref[b, i] > 0 for b in range(n_blocks)]
            any_read = functools.reduce(jnp.logical_or, reads)

            @pl.when(jnp.logical_and(any_read, count < read_most))
            def _():
                slot = owner_ref[i]
                column = jnp.bitwise_xor(lax.rem(slot, 4), lax.rem(me, 4))
                behind = lax.rem(lax.div(me, 4) - lax.div(slot, 4) + n, n)
                place[count] = column * n + behind
                for b in range(n_blocks):
                    bias[b, count] = jnp.where(reads[b], 0.0, -1e30).astype(F32)

            return count + any_read.astype(jnp.int32)

        lax.fori_loop(0, n_images, look, jnp.int32(0))

    for a in range(4):
        k_all[a * n : (a + 1) * n] = k_cols[a][...]
        v_all[a * n : (a + 1) * n] = v_cols[a][...]
    for j in range(read_most):
        rows = slice(j * img_tok, (j + 1) * img_tok)
        k_sel[rows] = k_all[place[j]]
        v_sel[rows] = v_all[place[j]]
    kt_sel[...] = k_sel[...].astype(F32).T.astype(BF16)
    dk_acc[...] = jnp.zeros_like(dk_acc)
    dv_acc[...] = jnp.zeros_like(dv_acc)

    pairs = groups // PAIR

    def one(it, carry):
        b = it // pairs
        g = it % pairs
        rows = pl.ds(pl.multiple_of(b * BLK, BLK), BLK)

        def heads_of(ref):
            return jnp.concatenate(
                [
                    ref[rows, pl.ds(pl.multiple_of((g * PAIR + u) * HD, HD), HD)]
                    for u in range(PAIR)
                ],
                axis=0,
            )

        query = heads_of(q_ref)
        cot = heads_of(cot_ref)
        scores = lax.dot_general(k_sel[...], query, NT, preferred_element_type=F32)
        scores = jnp.concatenate(
            [scores[j * img_tok : (j + 1) * img_tok] + bias[b, j] for j in range(read_most)],
            axis=0,
        )
        row_max = jnp.max(scores, axis=0, keepdims=True)
        terms = jnp.exp2((scores - row_max) * to_exp2)
        prob = terms * (1.0 / jnp.sum(terms, axis=0, keepdims=True))
        prob_half = prob.astype(BF16)
        prob_grad = lax.dot_general(v_sel[...], cot, NT, preferred_element_type=F32)
        delta = jnp.sum(prob_half.astype(F32) * prob_grad, axis=0, keepdims=True)
        score_grad = (prob * (prob_grad - delta)).astype(BF16)
        dq_t = jnp.dot(kt_sel[...], score_grad, preferred_element_type=F32)
        dq = (dq_t.T * (gate_value * inv_root)).astype(BF16)
        for u in range(PAIR):
            lanes = pl.ds(pl.multiple_of((g * PAIR + u) * HD, HD), HD)
            dq_ref[rows, lanes] = dq[u * BLK : (u + 1) * BLK]
        dk_acc[...] += jnp.dot(score_grad, query, preferred_element_type=F32)
        dv_acc[...] += jnp.dot(prob_half, cot, preferred_element_type=F32)
        gate_acc[0:1, :] += delta
        return carry

    lax.fori_loop(0, n_blocks * pairs, one, 0, unroll=UNROLL)

    dk_all[...] = jnp.zeros_like(dk_all)
    dv_all[...] = jnp.zeros_like(dv_all)
    for j in range(read_most):
        rows = slice(j * img_tok, (j + 1) * img_tok)
        dk_all[place[j]] = dk_acc[rows] * (gate_value * inv_root)
        dv_all[place[j]] = dv_acc[rows] * gate_value
    own_ref[:, :img_tok] = dk_all[0:n]
    own_ref[:, img_tok:] = dv_all[0:n]
    gate_row = sum(gate_acc[0:1, u * HD : (u + 1) * HD] for u in range(PAIR))
    gate_out[...] = jnp.broadcast_to(gate_row, gate_out.shape)
    if two_step:
        dk_x, dk_yd, dv_y, dv_xd = back_refs
        rest = 2 * n * img_tok
        dk_x[...] = dk_all[n : 2 * n]
        dk_yd[:rest] = dk_all[2 * n :].astype(BF16).reshape(rest, HD)
        last = step == pl.num_programs(0) - 1
        dk_yd[rest:] = coded(jnp.where(last, gate_row, 0.0), CODE, rounded_here)
        dv_y[...] = dv_all[2 * n : 3 * n]
        dv_xd[0:n] = dv_all[n : 2 * n].astype(BF16)
        dv_xd[n:] = dv_all[3 * n :].astype(BF16)
    else:
        for a in range(1, 4):
            back_refs[a - 1][:, :img_tok] = dk_all[a * n : (a + 1) * n].astype(BF16)
            back_refs[a - 1][:, img_tok:] = dv_all[a * n : (a + 1) * n].astype(BF16)


def attention(first, heads, n, two_step, prev_dq, gate_in, scalars, queries, cotangent, keys, values):
    tokens = queries.shape[0]
    total_kv = scalars[4]
    n_images = scalars[0].shape[1]
    img_tok = scalars[5]
    groups = queries.shape[1] // HD // total_kv
    width = groups * HD
    n_keys = n_images // 2 * img_tok
    smem = pl.BlockSpec(memory_space=pltpu.SMEM)
    wide = pl.BlockSpec((tokens, width), lambda i: (0, first + i))
    small = pl.BlockSpec((8, HD), lambda i: (0, 0))

    def cols(shape, place=(0, 0)):
        return pl.BlockSpec((*shape, HD), lambda i: (*place, i))

    in_specs = [smem] * 4 + [small, wide, wide]
    args = [*scalars[:4], gate_in, queries, cotangent]
    for array, place in (*keys, *values):
        in_specs.append(cols((n, img_tok), place))
        args.append(array)
    aliases = {}
    if prev_dq is not None:
        aliases[len(args)] = 0
        in_specs.append(pl.BlockSpec(memory_space=pl.ANY))
        args.append(prev_dq)
    span = heads * HD
    outs = [((n, 2 * img_tok), F32)]
    if two_step:
        outs += [((n, img_tok), F32), ((2 * n * img_tok + CODE,), BF16)]
        outs += [((n, img_tok), F32), ((2 * n, img_tok), BF16)]
    else:
        outs += [((n, 2 * img_tok), BF16)] * 3
    out_shape = [jax.ShapeDtypeStruct(queries.shape, BF16)]
    out_shape += [jax.ShapeDtypeStruct((*shape, span), kind) for shape, kind in outs]
    out_shape.append(jax.ShapeDtypeStruct((8, HD), F32))
    out_specs = [wide] + [cols(shape, (0,) * len(shape)) for shape, kind in outs] + [small]
    rows = tokens * groups * heads
    return pl.pallas_call(
        functools.partial(attention_kernel, n, two_step, len(aliases)),
        grid=(heads,),
        in_specs=in_specs,
        out_specs=out_specs,
        out_shape=out_shape,
        input_output_aliases=aliases,
        scratch_shapes=[
            pltpu.VMEM((4 * n, img_tok, HD), BF16),
            pltpu.VMEM((4 * n, img_tok, HD), BF16),
            pltpu.VMEM((n_keys, HD), BF16),
            pltpu.VMEM((n_keys, HD), BF16),
            pltpu.VMEM((HD, n_keys), BF16),
            pltpu.VMEM((n_keys, HD), F32),
            pltpu.VMEM((n_keys, HD), F32),
            pltpu.VMEM((4 * n, img_tok, HD), F32),
            pltpu.VMEM((4 * n, img_tok, HD), F32),
            pltpu.VMEM((8, PAIR * BLK), F32),
            pltpu.SMEM((n_images // 2,), jnp.int32),
            pltpu.SMEM((scalars[0].shape[0], n_images // 2), F32),
        ],
        compiler_params=pltpu.CompilerParams(
            dimension_semantics=("arbitrary",),
            vmem_limit_bytes=(14 + 16 * n_keys // 1024) * 1024 * 1024,
        ),
        cost_estimate=pl.CostEstimate(
            flops=10 * rows * n_keys * HD,
            bytes_accessed=6 * rows * HD,
            transcendentals=rows * n_keys,
        ),
        name="attention_backward",
    )(*args)


def per_device(queries, cotangent, image_keys, image_values, attn_gate, block_mask, image_owner):
    n_ctx = lax.axis_size("ctx")
    n_tp = lax.axis_size("tp")
    n = n_ctx // 4
    img_tok = image_keys.shape[1]
    local_kv = image_keys.shape[2] // HD
    chunks = min(CHUNKS, local_kv)
    heads = local_kv // chunks
    me = lax.axis_index("ctx").astype(jnp.int32).reshape(1)
    gate_value = jnp.tanh(attn_gate)

    def swap(value, bit):
        return lax.ppermute(value, "ctx", [(i, i ^ bit) for i in range(n_ctx)])

    def turn(value, by):
        pairs = [(i, (i // 4 + by) % n * 4 + i % 4) for i in range(n_ctx)]
        return lax.ppermute(value, "ctx", pairs)

    def fetch_column(c):
        lanes = slice(c * heads * HD, (c + 1) * heads * HD)
        own = jnp.concatenate([image_keys[0, :, lanes], image_values[0, :, lanes]], axis=0)
        return jnp.stack([own] + [turn(own, k) for k in range(1, n)])

    def fetch_two_step(column):
        k_own, v_own = column[:, :img_tok], column[:, img_tok:]
        k_x, v_y = swap(k_own, 1), swap(v_own, 2)
        k_yd = swap(jnp.concatenate([k_own, k_x]), 2)
        v_xd = swap(jnp.concatenate([v_own, v_y]), 1)
        first, second = (0, 0), (1, 0)
        keys = [(column, (0, 0)), (k_x, first), (k_yd, first), (k_yd, second)]
        values = [(column, (0, 1)), (v_xd, first), (v_y, first), (v_xd, second)]
        return keys, values

    def fetch_direct(column):
        columns = [column, swap(column, 1), swap(column, 2), swap(column, 3)]
        return [(part, (0, 0)) for part in columns], [(part, (0, 1)) for part in columns]

    def return_direct(own, backs):
        total = own
        for a, back in enumerate(backs):
            total = total + swap(back, a + 1).astype(F32)
        return total, None

    def return_two_step(own, backs):
        dk_x, dk_yd, dv_y, dv_xd = backs
        rest = 2 * n * img_tok
        width = own.shape[2]
        k_back, v_back = swap(dk_yd, 2), swap(dv_xd, 1)
        gate = decoded(dk_yd[rest:]) + decoded(k_back[rest:])
        k_back = k_back[:rest].reshape(2 * n, img_tok, width)
        k_send = (dk_x + k_back[n:].astype(F32)).astype(BF16).reshape(n * img_tok, width)
        v_send = (dv_y + v_back[n:].astype(F32)).astype(BF16)
        k_last = swap(jnp.concatenate([k_send, coded(gate, CODE, rounded_outside)]), 1)
        v_last = swap(v_send, 2)
        gate = gate + decoded(k_last[n * img_tok :])
        k_last = k_last[: n * img_tok].reshape(n, img_tok, width)
        k_sum = own[:, :img_tok] + k_back[:n].astype(F32) + k_last.astype(F32)
        v_sum = own[:, img_tok:] + v_back[:n].astype(F32) + v_last.astype(F32)
        return jnp.concatenate([k_sum, v_sum], axis=1), gate

    def return_column(both, gate):
        total, gate_total = both[0], gate
        sends = both.astype(BF16)
        for k in range(1, n):
            send = sends[k]
            if gate is not None:
                send = jnp.concatenate([send, coded(gate, CODE, rounded_outside)])
            came = turn(send, -k)
            total = total + came[: 2 * img_tok].astype(F32)
            if gate is not None:
                gate_total = gate_total + decoded(came[2 * img_tok :])
        return total, gate_total

    columns = [fetch_column(c) for c in range(chunks)]
    gathered = [(fetch_two_step if c == 0 else fetch_direct)(columns[c]) for c in range(chunks)]
    scalars = (block_mask, image_owner, me, gate_value, local_kv, img_tok)
    dq, gate_part = None, jnp.zeros((8, HD), F32)
    parts = []
    for c in range(chunks):
        last = c == chunks - 1
        keys, values = gathered[c]
        dq, own, *backs, gate_part = attention(
            c * heads, heads, n, last, dq, gate_part, scalars, queries, cotangent, keys, values
        )
        sums = return_two_step(own, backs) if last else return_direct(own, backs)
        total, gate_row = return_column(*sums)
        parts.append(total.astype(BF16))
    grads = jnp.concatenate(parts, axis=1)
    key_grad, value_grad = grads[None, :img_tok], grads[None, img_tok:]
    gate_total = gate_row
    for k in range(1, n_tp):
        pairs = [(i, (i + k) % n_tp) for i in range(n_tp)]
        gate_total = gate_total + lax.ppermute(gate_row, "tp", pairs)
    term_count = queries.shape[0] * n_ctx * queries.shape[1] * n_tp
    gate_grad = (1.0 - gate_value * gate_value) * jnp.sum(gate_total) / math.sqrt(term_count)
    return (dq, key_grad, value_grad, gate_grad)


def solution(mesh):
    in_specs = (
        P("ctx", "tp"),
        P("ctx", "tp"),
        P("ctx", None, "tp"),
        P("ctx", None, "tp"),
        P(),
        P("ctx", None),
        P(),
    )
    out_specs = (P("ctx", "tp"), P("ctx", None, "tp"), P("ctx", None, "tp"), P())
    return jax.shard_map(
        per_device, mesh=mesh, in_specs=in_specs, out_specs=out_specs, check_vma=False
    )
```

```python
import functools
import math

import jax
import jax.numpy as jnp
from jax import lax
from jax.experimental import pallas as pl
from jax.experimental.pallas import tpu as pltpu
from jax.sharding import PartitionSpec as P

HD = 128
BLK = 128
PAIR = 2
CHUNKS = 2
VMEM_MB = 48
CODE = 16
NT = (((1,), (1,)), ((), ()))
F32, BF16 = jnp.float32, jnp.bfloat16


def coded(value, rows, rounded):
    high = rounded(value)
    middle = rounded(value - high)
    low = value - high - middle
    shape = (rows, value.shape[1])
    row = lax.broadcasted_iota(jnp.int32, shape, 0)
    parts = jnp.where(row == 0, high, jnp.zeros(shape, F32))
    return jnp.where(row == 1, middle, jnp.where(row == 2, low, parts)).astype(BF16)


def rounded_here(value):
    return value.astype(BF16).astype(F32)


def rounded_outside(value):
    return lax.reduce_precision(value, 8, 7)


def decoded(rows):
    rows = rows.astype(F32)
    return rows[0:1] + rows[1:2] + rows[2:3]


def attention_kernel(n, n_blocks, n_images, z_last, first, heads, n_arrays, n_extra, *refs):
    plan_ref, gate_ref, gate_in, q_hbm, cot_hbm = refs[:5]
    columns = refs[5 : 5 + n_arrays]
    refs = refs[5 + n_arrays + n_extra :]
    dq_hbm, own_ref = refs[:2]
    back_refs = refs[2:5]
    (
        gate_out,
        q_ref,
        cot_ref,
        dq_ref,
        k_all,
        v_all,
        k_sel,
        v_sel,
        kt_sel,
        dk_acc,
        dv_acc,
        dk_all,
        dv_all,
        gate_acc,
        fetch_place,
        back_place,
        bias,
        in_sem,
        out_sem,
    ) = refs[5:]
    img_tok = k_all.shape[2]
    read_most = n_images // 2
    width = q_ref.shape[2]
    groups = width // HD
    gate_value = gate_ref[0]
    inv_root = 1.0 / math.sqrt(HD)
    to_exp2 = math.log2(math.e) * inv_root

    def span(h):
        return pl.ds((first + h) * width, width)

    copies = []
    for h in range(heads):
        q_copy = pltpu.make_async_copy(q_hbm.at[:, span(h)], q_ref.at[h], in_sem.at[0, h])
        cot_copy = pltpu.make_async_copy(cot_hbm.at[:, span(h)], cot_ref.at[h], in_sem.at[1, h])
        copies.append((q_copy, cot_copy))
    for copy in copies[0]:
        copy.start()

    gate_acc[...] = jnp.zeros_like(gate_acc)
    gate_acc[0:1, 0:HD] = gate_in[0:1, :]
    me = plan_ref[(n_blocks + 1) * n_images]
    for j in range(read_most):
        fetch_place[j] = 0
        back_place[j] = 0
        for b in range(n_blocks):
            bias[b, j] = jnp.float32(-1e30)

    def look(i, count):
        reads = [plan_ref[b * n_images + i] > 0 for b in range(n_blocks)]
        any_read = functools.reduce(jnp.logical_or, reads)

        @pl.when(jnp.logical_and(any_read, count < read_most))
        def _():
            slot = plan_ref[n_blocks * n_images + i]
            column = jnp.bitwise_xor(lax.rem(slot, 4), lax.rem(me, 4))
            behind = lax.rem(lax.div(me, 4) - lax.div(slot, 4) + n, n)
            back_place[count] = column * n + behind
            fetch_place[count] = behind * 4 + column if z_last else column * n + behind
            for b in range(n_blocks):
                bias[b, count] = jnp.where(reads[b], 0.0, -1e30).astype(F32)

        return count + any_read.astype(jnp.int32)

    lax.fori_loop(0, n_images, look, jnp.int32(0))

    def select(h):
        lanes = slice(h * HD, (h + 1) * HD)
        at = 0
        for column in columns:
            count = column.shape[0]
            k_all[h, at : at + count] = column[:, :img_tok, lanes]
            v_all[h, at : at + count] = column[:, img_tok:, lanes]
            at += count
        for j in range(read_most):
            rows = slice(j * img_tok, (j + 1) * img_tok)
            k_sel[h, rows] = k_all[h, fetch_place[j]]
            v_sel[h, rows] = v_all[h, fetch_place[j]]
        kt_sel[h] = k_sel[h].astype(F32).T.astype(BF16)
        dk_acc[h] = jnp.zeros_like(dk_acc[h])
        dv_acc[h] = jnp.zeros_like(dv_acc[h])

    pairs = groups // PAIR

    def heads_of(ref, h, rows, g):
        lanes = [slice((g * PAIR + u) * HD, (g * PAIR + u + 1) * HD) for u in range(PAIR)]
        return jnp.concatenate([ref[h, rows, lane] for lane in lanes], axis=0)

    def products(item):
        h, b, g = item
        rows = slice(b * BLK, (b + 1) * BLK)
        query, cot = heads_of(q_ref, h, rows, g), heads_of(cot_ref, h, rows, g)
        scores = lax.dot_general(k_sel[h], query, NT, preferred_element_type=F32)
        prob_grad = lax.dot_general(v_sel[h], cot, NT, preferred_element_type=F32)
        return scores, prob_grad

    def softmax(item, scores, prob_grad):
        h, b, g = item
        scores = jnp.concatenate(
            [scores[j * img_tok : (j + 1) * img_tok] + bias[b, j] for j in range(read_most)],
            axis=0,
        )
        row_max = jnp.max(scores, axis=0, keepdims=True)
        terms = jnp.exp2((scores - row_max) * to_exp2)
        prob = terms * (1.0 / jnp.sum(terms, axis=0, keepdims=True))
        prob_half = prob.astype(BF16)
        delta = jnp.sum(prob_half.astype(F32) * prob_grad, axis=0, keepdims=True)
        score_grad = (prob * (prob_grad - delta)).astype(BF16)
        gate_acc[0:1, :] += delta
        return prob_half, score_grad

    def gradients(item, prob_half, score_grad):
        h, b, g = item
        rows = slice(b * BLK, (b + 1) * BLK)
        query, cot = heads_of(q_ref, h, rows, g), heads_of(cot_ref, h, rows, g)
        dq_t = jnp.dot(kt_sel[h], score_grad, preferred_element_type=F32)
        dq = (dq_t.T * (gate_value * inv_root)).astype(BF16)
        for u in range(PAIR):
            lanes = slice((g * PAIR + u) * HD, (g * PAIR + u + 1) * HD)
            dq_ref[h, rows, lanes] = dq[u * BLK : (u + 1) * BLK]
        dk_acc[h] += jnp.dot(score_grad, query, preferred_element_type=F32)
        dv_acc[h] += jnp.dot(prob_half, cot, preferred_element_type=F32)

    def finish(h):
        lanes = slice(h * HD, (h + 1) * HD)
        out_copies.append(
            pltpu.make_async_copy(dq_ref.at[h], dq_hbm.at[:, span(h)], out_sem.at[h])
        )
        out_copies[-1].start()
        dk_all[h] = jnp.zeros_like(dk_all[h])
        dv_all[h] = jnp.zeros_like(dv_all[h])
        for j in range(read_most):
            rows = slice(j * img_tok, (j + 1) * img_tok)
            dk_all[h, back_place[j]] = dk_acc[h, rows] * (gate_value * inv_root)
            dv_all[h, back_place[j]] = dv_acc[h, rows] * gate_value
        own_ref[:, :img_tok, lanes] = dk_all[h, 0:n]
        own_ref[:, img_tok:, lanes] = dv_all[h, 0:n]
        for a in range(1, 4):
            out, rows = back_refs[a - 1], 2 * img_tok
            for k in range(n):
                dk, dv = dk_all[h, a * n + k], dv_all[h, a * n + k]
                out[k * rows : k * rows + img_tok, lanes] = dk.astype(BF16)
                out[k * rows + img_tok : (k + 1) * rows, lanes] = dv.astype(BF16)

    out_copies = []
    items = [(h, b, g) for h in range(heads) for b in range(n_blocks) for g in range(pairs)]
    ready, done = None, None
    for at in range(len(items) + 2):
        fresh = None
        if at < len(items):
            h = items[at][0]
            if at == 0 or items[at - 1][0] != h:
                select(h)
                for copy in copies[h]:
                    copy.wait()
                if h + 1 < heads:
                    for copy in copies[h + 1]:
                        copy.start()
            fresh = (items[at], *products(items[at]))
        middle = None
        if ready is not None:
            middle = (ready[0], *softmax(*ready))
        if done is not None:
            gradients(*done)
            h = done[0][0]
            if done[0] == [item for item in items if item[0] == h][-1]:
                finish(h)
        ready, done = fresh, middle

    gate_row = sum(gate_acc[0:1, u * HD : (u + 1) * HD] for u in range(PAIR))
    gate_out[...] = jnp.broadcast_to(gate_row, gate_out.shape)
    rest = 2 * n * img_tok
    for out in back_refs:
        out[rest:] = jnp.zeros((CODE, heads * HD), BF16)
        out[rest:, :HD] = coded(gate_row, CODE, rounded_here)
    for copy in out_copies:
        copy.wait()


def attention(first, heads, n, z_last, prev_dq, gate_in, scalars, queries, cotangent, columns):
    tokens = queries.shape[0]
    plan, gate_value, n_blocks, n_images, total_kv = scalars
    img_tok = columns[0].shape[1] // 2
    groups = queries.shape[1] // HD // total_kv
    width = groups * HD
    n_keys = n_images // 2 * img_tok
    smem = pl.BlockSpec(memory_space=pltpu.SMEM)
    vmem = pl.BlockSpec(memory_space=pltpu.VMEM)
    hbm = pl.BlockSpec(memory_space=pltpu.HBM)

    span = heads * HD
    in_specs = [smem] * 2 + [vmem, hbm, hbm]
    args = [plan, gate_value, gate_in]
    args += [pltpu.with_memory_space_constraint(x, pltpu.HBM) for x in (queries, cotangent)]
    in_specs += [vmem] * len(columns)
    args += columns
    aliases = {}
    if prev_dq is not None:
        aliases[len(args)] = 0
        in_specs.append(hbm)
        args.append(prev_dq)
    outs = [((n, 2 * img_tok), F32)]
    outs += [((2 * n * img_tok + CODE,), BF16)] * 3
    out_shape = [pltpu.HBM(queries.shape, BF16)]
    out_shape += [jax.ShapeDtypeStruct((*shape, span), kind) for shape, kind in outs]
    out_shape.append(jax.ShapeDtypeStruct((8, HD), F32))
    rows = tokens * groups * heads
    return pl.pallas_call(
        functools.partial(attention_kernel, n, n_blocks, n_images, z_last, first, heads, len(columns), len(aliases)),
        in_specs=in_specs,
        out_specs=[hbm] + [vmem] * (len(out_shape) - 1),
        out_shape=out_shape,
        input_output_aliases=aliases,
        scratch_shapes=[
            pltpu.VMEM((heads, tokens, width), BF16),
            pltpu.VMEM((heads, tokens, width), BF16),
            pltpu.VMEM((heads, tokens, width), BF16),
            pltpu.VMEM((heads, 4 * n, img_tok, HD), BF16),
            pltpu.VMEM((heads, 4 * n, img_tok, HD), BF16),
            pltpu.VMEM((heads, n_keys, HD), BF16),
            pltpu.VMEM((heads, n_keys, HD), BF16),
            pltpu.VMEM((heads, HD, n_keys), BF16),
            pltpu.VMEM((heads, n_keys, HD), F32),
            pltpu.VMEM((heads, n_keys, HD), F32),
            pltpu.VMEM((heads, 4 * n, img_tok, HD), F32),
            pltpu.VMEM((heads, 4 * n, img_tok, HD), F32),
            pltpu.VMEM((8, PAIR * BLK), F32),
            pltpu.SMEM((n_images // 2,), jnp.int32),
            pltpu.SMEM((n_images // 2,), jnp.int32),
            pltpu.SMEM((n_blocks, n_images // 2), F32),
            pltpu.SemaphoreType.DMA((2, heads)),
            pltpu.SemaphoreType.DMA((heads,)),
        ],
        compiler_params=pltpu.CompilerParams(
            vmem_limit_bytes=VMEM_MB * 1024 * 1024,
        ),
        cost_estimate=pl.CostEstimate(
            flops=10 * rows * n_keys * HD,
            bytes_accessed=6 * rows * HD,
            transcendentals=rows * n_keys,
        ),
        name="attention_backward",
    )(*args)


def per_device(queries, cotangent, image_keys, image_values, attn_gate, block_mask, image_owner):
    n_ctx = lax.axis_size("ctx")
    n_tp = lax.axis_size("tp")
    n = n_ctx // 4
    img_tok = image_keys.shape[1]
    local_kv = image_keys.shape[2] // HD
    chunks = min(CHUNKS, local_kv)
    heads = local_kv // chunks
    me = lax.axis_index("ctx").astype(jnp.int32).reshape(1)
    plan = jnp.concatenate([block_mask.reshape(-1), image_owner, me])
    gate_value = jnp.tanh(attn_gate)

    def swap(value, bit):
        return lax.ppermute(value, "ctx", [(i, i ^ bit) for i in range(n_ctx)])

    def turn(value, by):
        pairs = [(i, (i // 4 + by) % n * 4 + i % 4) for i in range(n_ctx)]
        return lax.ppermute(value, "ctx", pairs)

    def own_columns(c):
        lanes = slice(c * heads * HD, (c + 1) * heads * HD)
        return jnp.concatenate([image_keys[0, :, lanes], image_values[0, :, lanes]], axis=0)

    def square_of(own):
        return jnp.stack([own, swap(own, 1), swap(own, 2), swap(own, 3)])

    def column_of(own):
        return jnp.stack([own] + [turn(own, k) for k in range(1, n)])

    def return_square(own, backs):
        rest = 2 * n * img_tok
        total, gate = own, decoded(backs[0][rest:])
        for a, back in enumerate(backs):
            came = swap(back, a + 1)
            total = total + came[:rest].reshape(own.shape).astype(F32)
            gate = gate + decoded(came[rest:])
        return total, gate

    def return_column(both, gate, last):
        total, gate_total = both[0], gate
        sends = both.astype(BF16)
        for k in range(1, n):
            send = sends[k]
            if last:
                send = jnp.concatenate([send, coded(gate, CODE, rounded_outside)])
            came = turn(send, -k)
            total = total + came[: 2 * img_tok].astype(F32)
            if last:
                gate_total = gate_total + decoded(came[2 * img_tok :])
        return total, gate_total

    owns = [own_columns(c) for c in range(chunks)]
    starts = [square_of(own) if c else column_of(own) for c, own in enumerate(owns)]
    if chunks > 1:
        starts = lax.optimization_barrier(starts)
    column = starts[0]
    gathered = [[column, swap(column, 1), swap(column, 2), swap(column, 3)]]
    for square in starts[1:]:
        gathered.append([square] + [turn(square, k) for k in range(1, n)])
    scalars = (plan, gate_value, *block_mask.shape, local_kv)
    dq, gate_part = None, jnp.zeros((8, HD), F32)
    parts = []
    for c in range(chunks):
        dq, own, *backs, gate_part = attention(
            c * heads, heads, n, c > 0, dq, gate_part, scalars, queries, cotangent, gathered[c]
        )
        total, gate_row = return_column(*return_square(own, backs), c == chunks - 1)
        parts.append(total.astype(BF16))
    grads = jnp.concatenate(parts, axis=1)
    key_grad, value_grad = grads[None, :img_tok], grads[None, img_tok:]
    gate_total = gate_row
    for k in range(1, n_tp):
        pairs = [(i, (i + k) % n_tp) for i in range(n_tp)]
        gate_total = gate_total + lax.ppermute(gate_row, "tp", pairs)
    term_count = queries.shape[0] * n_ctx * queries.shape[1] * n_tp
    gate_grad = (1.0 - gate_value * gate_value) * jnp.sum(gate_total) / math.sqrt(term_count)
    return (dq, key_grad, value_grad, gate_grad)


def solution(mesh):
    in_specs = (
        P("ctx", "tp"),
        P("ctx", "tp"),
        P("ctx", None, "tp"),
        P("ctx", None, "tp"),
        P(),
        P("ctx", None),
        P(),
    )
    out_specs = (P("ctx", "tp"), P("ctx", None, "tp"), P("ctx", None, "tp"), P())
    return jax.shard_map(
        per_device, mesh=mesh, in_specs=in_specs, out_specs=out_specs, check_vma=False
    )
```

```python
import functools
import math

import jax
import jax.numpy as jnp
from jax import lax
from jax.experimental import pallas as pl
from jax.experimental.pallas import tpu as pltpu
from jax.sharding import PartitionSpec as P

HD = 128
BLK = 128
JOIN = 4
FIRST = 0
MERGE = 2
CHUNKS = 2
CODE = 16
NT = (((1,), (1,)), ((), ()))
F32, BF16 = jnp.float32, jnp.bfloat16


def coded(value, rows, rounded):
    high = rounded(value)
    middle = rounded(value - high)
    low = value - high - middle
    shape = (rows, value.shape[1])
    row = lax.broadcasted_iota(jnp.int32, shape, 0)
    parts = jnp.where(row == 0, high, jnp.zeros(shape, F32))
    return jnp.where(row == 1, middle, jnp.where(row == 2, low, parts)).astype(BF16)


def rounded_here(value):
    return value.astype(BF16).astype(F32)


def rounded_outside(value):
    return lax.reduce_precision(value, 8, 7)


def decoded(rows):
    rows = rows.astype(F32)
    return rows[0:1] + rows[1:2] + rows[2:3]


def plan_images(n, n_blocks, n_images, plan_ref, place, bias):
    read_most = n_images // 2
    me = plan_ref[(n_blocks + 1) * n_images]
    for j in range(read_most):
        place[0, j] = 0
        place[1, j] = 0
        for b in range(n_blocks):
            bias[b, j] = jnp.float32(-1e30)

    def look(i, count):
        reads = [plan_ref[b * n_images + i] > 0 for b in range(n_blocks)]
        any_read = functools.reduce(jnp.logical_or, reads)

        @pl.when(jnp.logical_and(any_read, count < read_most))
        def _():
            slot = plan_ref[n_blocks * n_images + i]
            column = jnp.bitwise_xor(lax.rem(slot, 4), lax.rem(me, 4))
            behind = lax.rem(lax.div(me, 4) - lax.div(slot, 4) + n, n)
            place[0, count] = column * n + behind
            place[1, count] = behind * 4 + column
            for b in range(n_blocks):
                bias[b, count] = jnp.where(reads[b], 0.0, -1e30).astype(F32)

        return count + any_read.astype(jnp.int32)

    lax.fori_loop(0, n_images, look, jnp.int32(0))


def attention_kernel(n, n_blocks, n_images, lead, first, heads, total_kv, n_columns, *refs):
    gate_ref, gate_in = refs[:2]
    columns = refs[2 : 2 + n_columns]
    refs = refs[2 + n_columns :]
    if lead:
        plan_ref, q_hbm, cot_hbm, place, bias, q_ref, cot_ref = refs[:7]
    else:
        place, bias, q_ref, cot_ref = refs[:4]
    refs = refs[7 if lead else 4 :]
    ds_ref, kt_sel, own_ref = refs[:3]
    back_refs = refs[3:6]
    gate_out, k_all, v_all, k_sel, v_sel, dk_acc, dv_acc, dk_all, dv_all, sem = refs[6:]
    read_most = n_images // 2
    img_tok = k_all.shape[2]
    per_head = ds_ref.shape[1]
    groups = per_head // n_blocks
    width = groups * HD
    gate_value = gate_ref[0]
    inv_root = 1.0 / math.sqrt(HD)
    to_exp2 = math.log2(math.e) * inv_root

    copies = []
    if lead:
        edges = [h * width for h in range(heads + 1)] + [total_kv * width]
        for k in range(heads + 1):
            span = slice(edges[k], edges[k + 1])
            if edges[k + 1] > edges[k]:
                for u, (src, dst) in enumerate(((q_hbm, q_ref), (cot_hbm, cot_ref))):
                    copies.append(
                        pltpu.make_async_copy(src.at[:, span], dst.at[:, span], sem.at[k, u])
                    )
                    copies[-1].start()
        plan_images(n, n_blocks, n_images, plan_ref, place, bias)

    for h in range(heads):
        lanes = slice(h * HD, (h + 1) * HD)
        at = 0
        for column in columns:
            count = column.shape[0]
            k_all[h, at : at + count] = column[:, :img_tok, lanes]
            v_all[h, at : at + count] = column[:, img_tok:, lanes]
            at += count
        for j in range(read_most):
            rows = slice(j * img_tok, (j + 1) * img_tok)
            where = place[0 if lead else 1, j]
            k_sel[h, rows] = k_all[h, where]
            v_sel[h, rows] = v_all[h, where]
        kt_sel[h] = k_sel[h].astype(F32).T.astype(BF16)
    dk_acc[...] = jnp.zeros_like(dk_acc)
    dv_acc[...] = jnp.zeros_like(dv_acc)

    def tile_of(ref, i):
        h, b, g = i // per_head, i % per_head // groups, i % groups
        lane = ((first + h) * groups + g) * HD
        return ref[b * BLK : (b + 1) * BLK, lane : lane + HD]

    def products(i):
        h = i // per_head
        scores = lax.dot_general(k_sel[h], tile_of(q_ref, i), NT, preferred_element_type=F32)
        prob_grad = lax.dot_general(v_sel[h], tile_of(cot_ref, i), NT, preferred_element_type=F32)
        return scores, prob_grad

    def softmax(i, scores, prob_grad):
        h, b = i // per_head, i % per_head // groups
        images = [scores[j * img_tok : (j + 1) * img_tok] for j in range(read_most)]
        tops = [
            jnp.max(image.reshape(img_tok // 8, 8, BLK), axis=0) + bias[b, j]
            for j, image in enumerate(images)
        ]
        row_max = jnp.max(functools.reduce(jnp.maximum, tops), axis=0, keepdims=True)
        terms = [
            jnp.exp2((image - (row_max - bias[b, j])) * to_exp2) for j, image in enumerate(images)
        ]
        terms = jnp.concatenate(terms, axis=0)
        prob = terms * (1.0 / jnp.sum(terms, axis=0, keepdims=True))
        delta = jnp.sum(prob * prob_grad, axis=0, keepdims=True)
        score_grad = (prob * (prob_grad - delta)).astype(BF16)
        ds_ref[h, i % per_head] = score_grad
        return prob.astype(BF16), score_grad

    def gradients(pieces):
        h = pieces[0][0] // per_head
        query = jnp.concatenate([tile_of(q_ref, i) for i, _, _ in pieces], axis=0)
        cot = jnp.concatenate([tile_of(cot_ref, i) for i, _, _ in pieces], axis=0)
        prob_half = jnp.concatenate([p for _, p, _ in pieces], axis=1)
        score_grad = jnp.concatenate([d for _, _, d in pieces], axis=1)
        dk_acc[h] += jnp.dot(score_grad, query, preferred_element_type=F32)
        dv_acc[h] += jnp.dot(prob_half, cot, preferred_element_type=F32)

    items = heads * per_head
    ready, held = None, []
    for at in range(items + 2):
        if at < items and at % per_head == 0:
            for copy in copies[2 * (at // per_head) : 2 * (at // per_head) + 2]:
                copy.wait()
        fresh = products(at) if at < items else None
        middle = (at - 1, *softmax(at - 1, *ready)) if ready is not None else None
        if len(held) == MERGE:
            gradients(held)
            held = []
        if middle is not None:
            held.append(middle)
        ready = fresh

    gate_row = jnp.zeros((1, HD), F32)
    for h in range(heads):
        lanes = slice(h * HD, (h + 1) * HD)
        dk_all[h] = jnp.zeros_like(dk_all[h])
        dv_all[h] = jnp.zeros_like(dv_all[h])
        for j in range(read_most):
            rows = slice(j * img_tok, (j + 1) * img_tok)
            dk_all[h, place[0, j]] = dk_acc[h, rows] * (gate_value * inv_root)
            dv_all[h, place[0, j]] = dv_acc[h, rows] * gate_value
        own_ref[:, :img_tok, lanes] = dk_all[h, 0:n]
        own_ref[:, img_tok:, lanes] = dv_all[h, 0:n]
        for a in range(1, 4):
            out, rows = back_refs[a - 1], 2 * img_tok
            for k in range(n):
                dk, dv = dk_all[h, a * n + k], dv_all[h, a * n + k]
                out[k * rows : k * rows + img_tok, lanes] = dk.astype(BF16)
                out[k * rows + img_tok : (k + 1) * rows, lanes] = dv.astype(BF16)
        gate_row += jnp.sum(dv_acc[h] * v_sel[h].astype(F32), axis=0, keepdims=True)
    gate_row = jnp.broadcast_to(jnp.sum(gate_row, axis=1, keepdims=True), (1, HD))
    gate_row += gate_in[0:1]
    gate_out[...] = jnp.broadcast_to(gate_row, gate_out.shape)
    rest = 2 * n * img_tok
    for out in back_refs:
        for h in range(heads):
            lanes = slice(h * HD, (h + 1) * HD)
            out[rest:, lanes] = coded(gate_row, CODE, rounded_here)
    for copy in copies[2 * heads :]:
        copy.wait()


def attention(at, sizes, gate_value, gate_in, columns, lead_in, shared):
    n, n_blocks, n_images, heads, total_kv, tokens = sizes
    lead = shared is None
    read_most = n_images // 2
    img_tok = columns[0].shape[1] // 2
    queries = lead_in[1]
    groups = queries.shape[1] // HD // total_kv
    per_head = groups * n_blocks
    n_keys = read_most * img_tok
    smem = pl.BlockSpec(memory_space=pltpu.SMEM)
    vmem = pl.BlockSpec(memory_space=pltpu.VMEM)
    hbm = pl.BlockSpec(memory_space=pltpu.HBM)
    span = heads * HD
    args = [gate_value, gate_in, *columns]
    in_specs = [smem] + [vmem] * (1 + len(columns))
    out_shape, out_specs = [], []
    if lead:
        args.append(lead_in[0])
        args += [pltpu.with_memory_space_constraint(x, pltpu.HBM) for x in lead_in[1:]]
        in_specs += [smem, hbm, hbm]
        out_shape += [
            jax.ShapeDtypeStruct((2, read_most), jnp.int32),
            jax.ShapeDtypeStruct((n_blocks, read_most), F32),
            pltpu.VMEM(queries.shape, BF16),
            pltpu.VMEM(queries.shape, BF16),
        ]
        out_specs += [smem, smem, vmem, vmem]
    else:
        args += shared
        in_specs += [smem, smem, vmem, vmem]
    tail_shape = [
        pltpu.VMEM((heads, per_head, n_keys, BLK), BF16),
        pltpu.VMEM((heads, HD, n_keys), BF16),
        jax.ShapeDtypeStruct((n, 2 * img_tok, span), F32),
    ]
    tail_shape += [jax.ShapeDtypeStruct((2 * n * img_tok + CODE, span), BF16)] * 3
    tail_shape.append(jax.ShapeDtypeStruct((8, HD), F32))
    out_shape += tail_shape
    out_specs += [vmem] * len(tail_shape)
    rows = tokens * groups * heads
    kernel = functools.partial(
        attention_kernel, n, n_blocks, n_images, lead, at * heads, heads, total_kv, len(columns)
    )
    return pl.pallas_call(
        kernel,
        in_specs=in_specs,
        out_specs=out_specs,
        out_shape=out_shape,
        scratch_shapes=[
            pltpu.VMEM((heads, 4 * n, img_tok, HD), BF16),
            pltpu.VMEM((heads, 4 * n, img_tok, HD), BF16),
            pltpu.VMEM((heads, n_keys, HD), BF16),
            pltpu.VMEM((heads, n_keys, HD), BF16),
            pltpu.VMEM((heads, n_keys, HD), F32),
            pltpu.VMEM((heads, n_keys, HD), F32),
            pltpu.VMEM((heads, 4 * n, img_tok, HD), F32),
            pltpu.VMEM((heads, 4 * n, img_tok, HD), F32),
            pltpu.SemaphoreType.DMA((heads + 1, 2)),
        ],
        compiler_params=pltpu.CompilerParams(vmem_limit_bytes=vmem_bytes(n_keys)),
        cost_estimate=pl.CostEstimate(
            flops=8 * rows * n_keys * HD,
            bytes_accessed=4 * rows * HD,
            transcendentals=rows * n_keys,
        ),
        name="attention_backward",
    )(*args)


def vmem_bytes(n_keys):
    return min(44, 14 + 15 * n_keys // 1024) * 1024 * 1024


def query_kernel(first, n_blocks, n_extra, gate_ref, ds_ref, kt_ref, *rest):
    dq_hbm, dq_ref, sem = rest[n_extra:]
    heads, per_head = ds_ref.shape[:2]
    groups = per_head // n_blocks
    width = groups * HD
    scale = gate_ref[0] * (1.0 / math.sqrt(HD))
    copies = []
    for h in range(heads):
        for i in range(0, per_head, JOIN):
            b, g = i // groups, i % groups
            score_grad = jnp.concatenate([ds_ref[h, i + u] for u in range(JOIN)], axis=1)
            dq = jnp.dot(kt_ref[h], score_grad, preferred_element_type=F32)
            dq = (dq.T * scale).astype(BF16)
            for u in range(JOIN):
                lanes = slice((g + u) * HD, (g + u + 1) * HD)
                dq_ref[h, b * BLK : (b + 1) * BLK, lanes] = dq[u * BLK : (u + 1) * BLK]
        span = pl.ds((first + h) * width, width)
        copies.append(pltpu.make_async_copy(dq_ref.at[h], dq_hbm.at[:, span], sem.at[h]))
        copies[-1].start()
    for copy in copies:
        copy.wait()


def query_gradient(at, sizes, shape, prev, after, gate_value, ds, kt):
    n, n_blocks, n_images, heads, total_kv, tokens = sizes
    hbm = pl.BlockSpec(memory_space=pltpu.HBM)
    vmem = pl.BlockSpec(memory_space=pltpu.VMEM)
    anywhere = pl.BlockSpec(memory_space=pl.ANY)
    extra = ([] if prev is None else [prev]) + after
    specs = ([] if prev is None else [hbm]) + [anywhere] * len(after)
    return pl.pallas_call(
        functools.partial(query_kernel, at * heads, n_blocks, len(extra)),
        in_specs=[pl.BlockSpec(memory_space=pltpu.SMEM), vmem, vmem] + specs,
        out_specs=hbm,
        out_shape=pltpu.HBM(shape, BF16),
        input_output_aliases={} if prev is None else {3: 0},
        scratch_shapes=[
            pltpu.VMEM((heads, shape[0], shape[1] // total_kv), BF16),
            pltpu.SemaphoreType.DMA((heads,)),
        ],
        compiler_params=pltpu.CompilerParams(vmem_limit_bytes=16 * 1024 * 1024),
        cost_estimate=pl.CostEstimate(
            flops=2 * ds.size * HD, bytes_accessed=2 * ds.size, transcendentals=0
        ),
        name="query_gradient",
    )(gate_value, ds, kt, *extra)


def per_device(queries, cotangent, image_keys, image_values, attn_gate, block_mask, image_owner):
    n_ctx = lax.axis_size("ctx")
    n_tp = lax.axis_size("tp")
    n = n_ctx // 4
    img_tok = image_keys.shape[1]
    local_kv = image_keys.shape[2] // HD
    chunks = min(CHUNKS, local_kv)
    heads = local_kv // chunks
    me = lax.axis_index("ctx").astype(jnp.int32).reshape(1)
    plan = jnp.concatenate([block_mask.reshape(-1), image_owner, me])
    gate_value = jnp.tanh(attn_gate)

    def swap(value, bit):
        return lax.ppermute(value, "ctx", [(i, i ^ bit) for i in range(n_ctx)])

    def turn(value, by):
        pairs = [(i, (i // 4 + by) % n * 4 + i % 4) for i in range(n_ctx)]
        return lax.ppermute(value, "ctx", pairs)

    def own_columns(c):
        lanes = slice(c * heads * HD, (c + 1) * heads * HD)
        return jnp.concatenate([image_keys[0, :, lanes], image_values[0, :, lanes]], axis=0)

    def square_of(own):
        pair = jnp.stack([own, swap(own, 1)])
        return jnp.concatenate([pair, swap(pair, 2)])

    def column_of(own):
        return jnp.stack([own] + [turn(own, k) for k in range(1, n)])

    def square_sum(own, backs, came):
        rest = 2 * n * img_tok
        total, gate = own, decoded(backs[0][rest:])
        for part in came:
            total = total + part[:rest].reshape(own.shape).astype(F32)
            gate = gate + decoded(part[rest:])
        return total, gate

    def return_column(both, gate, last):
        total, gate_total = both[0], gate
        sends = both.astype(BF16)
        for k in range(1, n):
            send = sends[k]
            if last:
                send = jnp.concatenate([send, coded(gate, CODE, rounded_outside)])
            came = turn(send, -k)
            total = total + came[: 2 * img_tok].astype(F32)
            if last:
                gate_total = gate_total + decoded(came[2 * img_tok :])
        return total, gate_total

    owns = [own_columns(c) for c in range(chunks)]
    starts = [square_of(own) if c else column_of(own) for c, own in enumerate(owns)]
    if chunks > 1:
        starts = lax.optimization_barrier(starts)
    column = starts[0]
    gathered = [[column, swap(column, 1), swap(column, 2), swap(column, 3)]]
    for square in starts[1:]:
        gathered.append([square] + [turn(square, k) for k in range(1, n)])
    sizes = (n, *block_mask.shape, heads, local_kv, queries.shape[0])
    lead_in = (plan, queries, cotangent)
    gate_part = jnp.zeros((8, HD), F32)
    shared, parts, dq = None, [], None
    saved, waiting = [], None
    for c in range(chunks):
        last = c == chunks - 1
        outs = attention(c, sizes, gate_value, gate_part, gathered[c], lead_in, shared)
        if shared is None:
            shared, outs = outs[:4], outs[4:]
        ds, kt, own, *backs, gate_part = outs
        saved.append((ds, kt))
        if c:
            held = lax.optimization_barrier((tuple(backs), waiting[2]))
            backs = held[0]
            both, gate = square_sum(waiting[0], waiting[1], held[1])
            total, gate_row = return_column(both, gate, False)
            parts.append(total.astype(BF16))
        came = [swap(back, a + 1) for a, back in enumerate(backs)]
        waiting = (own, backs, tuple(came))
        if last:
            for k, (ds, kt) in enumerate(saved):
                after = came[FIRST : FIRST + 1] if k == c else []
                dq = query_gradient(k, sizes, queries.shape, dq, after, gate_value, ds, kt)
            *came, dq = lax.optimization_barrier((*came, dq))
    both, gate = square_sum(own, backs, came)
    total, gate_row = return_column(both, gate, True)
    parts.append(total.astype(BF16))
    grads = jnp.concatenate(parts, axis=1)
    key_grad, value_grad = grads[None, :img_tok], grads[None, img_tok:]
    gate_total = gate_row
    for k in range(1, n_tp):
        pairs = [(i, (i + k) % n_tp) for i in range(n_tp)]
        gate_total = gate_total + lax.ppermute(gate_row, "tp", pairs)
    term_count = queries.shape[0] * n_ctx * queries.shape[1] * n_tp
    gate_row = gate_total[0, :HD] * (1.0 / math.sqrt(term_count))
    gate_grad = ((1.0 - gate_value * gate_value) * gate_row)[:1]
    return (dq, key_grad, value_grad, gate_grad)


def solution(mesh):
    in_specs = (
        P("ctx", "tp"),
        P("ctx", "tp"),
        P("ctx", None, "tp"),
        P("ctx", None, "tp"),
        P(),
        P("ctx", None),
        P(),
    )
    out_specs = (P("ctx", "tp"), P("ctx", None, "tp"), P("ctx", None, "tp"), P())
    return jax.shard_map(
        per_device, mesh=mesh, in_specs=in_specs, out_specs=out_specs, check_vma=False
    )
```

```python
import functools
import math

import jax
import jax.numpy as jnp
from jax import lax
from jax.experimental import pallas as pl
from jax.experimental.pallas import tpu as pltpu
from jax.sharding import PartitionSpec as P

HD = 128
BLK = 128
JOIN = 4
FIRST = 0
MERGE = 2
CHUNKS = 2
CODE = 16
NT = (((1,), (1,)), ((), ()))
F32, BF16 = jnp.float32, jnp.bfloat16


def coded(value, rows, rounded):
    high = rounded(value)
    middle = rounded(value - high)
    low = value - high - middle
    shape = (rows, value.shape[1])
    row = lax.broadcasted_iota(jnp.int32, shape, 0)
    parts = jnp.where(row == 0, high, jnp.zeros(shape, F32))
    return jnp.where(row == 1, middle, jnp.where(row == 2, low, parts)).astype(BF16)


def rounded_here(value):
    return value.astype(BF16).astype(F32)


def rounded_outside(value):
    return lax.reduce_precision(value, 8, 7)


def decoded(rows):
    rows = rows.astype(F32)
    return rows[0:1] + rows[1:2] + rows[2:3]


def plan_images(n, n_blocks, n_images, part_rows, plan_ref, place, bias):
    read_most = n_images // 2
    me = plan_ref[(n_blocks + 1) * n_images]
    for j in range(read_most):
        place[0, j] = 0
        place[1, j] = 0
        place[2, j] = 0
        for b in range(n_blocks):
            bias[b, j] = jnp.float32(-1e30)

    def look(i, count):
        reads = [plan_ref[b * n_images + i] > 0 for b in range(n_blocks)]
        any_read = functools.reduce(jnp.logical_or, reads)

        @pl.when(jnp.logical_and(any_read, count < read_most))
        def _():
            slot = plan_ref[n_blocks * n_images + i]
            column = jnp.bitwise_xor(lax.rem(slot, 4), lax.rem(me, 4))
            across = jnp.bitwise_xor(lax.div(slot, 4), lax.div(me, 4))
            place[0, count] = column * n + across
            place[1, count] = across * 4 + column
            place[2, count] = (column * n + across) * part_rows
            for b in range(n_blocks):
                bias[b, count] = jnp.where(reads[b], 0.0, -1e30).astype(F32)

        return count + any_read.astype(jnp.int32)

    lax.fori_loop(0, n_images, look, jnp.int32(0))


def prepare_kernel(n, n_blocks, n_images, part_rows, *refs):
    plan_ref, q_hbm, cot_hbm, _, place, bias, q_ref, cot_ref, sem = refs
    half = q_ref.shape[0] // 2
    copies = []
    for u, (src, dst) in enumerate(((q_hbm, q_ref), (cot_hbm, cot_ref))):
        for k in range(2):
            rows = slice(k * half, (k + 1) * half)
            copies.append(pltpu.make_async_copy(src.at[rows], dst.at[rows], sem.at[u, k]))
            copies[-1].start()
    plan_images(n, n_blocks, n_images, part_rows, plan_ref, place, bias)
    for copy in copies:
        copy.wait()


def prepare(sizes, img_tok, plan, queries, cotangent, after):
    n, n_blocks, n_images = sizes[:3]
    smem = pl.BlockSpec(memory_space=pltpu.SMEM)
    vmem = pl.BlockSpec(memory_space=pltpu.VMEM)
    hbm = pl.BlockSpec(memory_space=pltpu.HBM)
    wide = [pltpu.with_memory_space_constraint(x, pltpu.HBM) for x in (queries, cotangent)]
    return pl.pallas_call(
        functools.partial(prepare_kernel, n, n_blocks, n_images, 2 * img_tok),
        in_specs=[smem, hbm, hbm, pl.BlockSpec(memory_space=pl.ANY)],
        out_specs=[smem, smem, vmem, vmem],
        out_shape=[
            jax.ShapeDtypeStruct((3, n_images // 2), jnp.int32),
            jax.ShapeDtypeStruct((n_blocks, n_images // 2), F32),
            pltpu.VMEM(queries.shape, BF16),
            pltpu.VMEM(queries.shape, BF16),
        ],
        scratch_shapes=[pltpu.SemaphoreType.DMA((2, 2))],
        compiler_params=pltpu.CompilerParams(vmem_limit_bytes=4 * 1024 * 1024),
        cost_estimate=pl.CostEstimate(
            flops=0, bytes_accessed=8 * queries.size, transcendentals=0
        ),
        name="prepare",
    )(plan, *wide, after)


def attention_kernel(n, n_blocks, n_images, lead, first, heads, total_kv, n_columns, *refs):
    gate_ref, gate_in = refs[:2]
    columns = refs[2 : 2 + n_columns]
    refs = refs[2 + n_columns :]
    place, bias, q_ref, cot_ref = refs[:4]
    ds_ref, k_sel = refs[4:6]
    out_refs = refs[6:10]
    gate_out, out_ref, k_all, v_all, v_sel, dk_acc, dv_acc = refs[10:]
    read_most = n_images // 2
    img_tok = k_all.shape[2]
    per_head = ds_ref.shape[1]
    groups = per_head // n_blocks
    width = groups * HD
    gate_value = gate_ref[0]
    inv_root = 1.0 / math.sqrt(HD)
    to_exp2 = math.log2(math.e) * inv_root

    for h in range(heads):
        lanes = slice(h * HD, (h + 1) * HD)
        at = 0
        for column in columns:
            count = column.shape[0]
            k_all[h, at : at + count] = column[:, :img_tok, lanes]
            v_all[h, at : at + count] = column[:, img_tok:, lanes]
            at += count
        for j in range(read_most):
            rows = slice(j * img_tok, (j + 1) * img_tok)
            where = place[0 if lead else 1, j]
            k_sel[h, rows] = k_all[h, where]
            v_sel[h, rows] = v_all[h, where]
    out_ref[...] = jnp.zeros_like(out_ref)
    dk_acc[...] = jnp.zeros_like(dk_acc)
    dv_acc[...] = jnp.zeros_like(dv_acc)

    def tile_of(ref, i):
        h, b, g = i // per_head, i % per_head // groups, i % groups
        lane = ((first + h) * groups + g) * HD
        return ref[b * BLK : (b + 1) * BLK, lane : lane + HD]

    def score_product(i):
        h = i // per_head
        return lax.dot_general(k_sel[h], tile_of(q_ref, i), NT, preferred_element_type=F32)

    def value_product(i):
        h = i // per_head
        return lax.dot_general(v_sel[h], tile_of(cot_ref, i), NT, preferred_element_type=F32)

    def probabilities(i, scores):
        b = i % per_head // groups
        images = [scores[j * img_tok : (j + 1) * img_tok] for j in range(read_most)]
        tops = [
            jnp.max(image.reshape(img_tok // 8, 8, BLK), axis=0) + bias[b, j]
            for j, image in enumerate(images)
        ]
        row_max = jnp.max(functools.reduce(jnp.maximum, tops), axis=0, keepdims=True)
        terms = [
            jnp.exp2((image - (row_max - bias[b, j])) * to_exp2) for j, image in enumerate(images)
        ]
        terms = jnp.concatenate(terms, axis=0)
        return terms * (1.0 / jnp.sum(terms, axis=0, keepdims=True))

    def score_gradient(i, prob, prob_grad):
        delta = jnp.sum(prob * prob_grad, axis=0, keepdims=True)
        score_grad = (prob * (prob_grad - delta)).astype(BF16)
        ds_ref[i // per_head, i % per_head] = score_grad
        return prob.astype(BF16), score_grad

    def gradients(pieces):
        h = pieces[0][0] // per_head
        query = jnp.concatenate([tile_of(q_ref, i) for i, _, _ in pieces], axis=0)
        cot = jnp.concatenate([tile_of(cot_ref, i) for i, _, _ in pieces], axis=0)
        prob_half = jnp.concatenate([p for _, p, _ in pieces], axis=1)
        score_grad = jnp.concatenate([d for _, _, d in pieces], axis=1)
        dk_acc[h] += jnp.dot(score_grad, query, preferred_element_type=F32)
        dv_acc[h] += jnp.dot(prob_half, cot, preferred_element_type=F32)

    def finish(h):
        lanes = slice(h * HD, (h + 1) * HD)
        for j in range(read_most):
            rows = slice(j * img_tok, (j + 1) * img_tok)
            at = place[2, j]
            for u, (acc, scale) in enumerate(((dk_acc, gate_value * inv_root), (dv_acc, gate_value))):
                out_rows = pl.ds(pl.multiple_of(at + u * img_tok, 16), img_tok)
                out_ref[out_rows, lanes] = (acc[h, rows] * scale).astype(BF16)
        return jnp.sum(dv_acc[h] * v_sel[h].astype(F32), axis=0, keepdims=True)

    items = heads * per_head
    gate_row = jnp.zeros((1, HD), F32)
    ready, waiting, held = None, None, []
    for at in range(items + 3):
        scores = score_product(at) if at < items else None
        values = value_product(at - 1) if 0 < at <= items else None
        prob = probabilities(at - 1, ready) if ready is not None else None
        middle = (at - 2, *score_gradient(at - 2, *waiting)) if waiting is not None else None
        if len(held) == MERGE:
            gradients(held)
            if (held[-1][0] + 1) % per_head == 0:
                gate_row += finish(held[-1][0] // per_head)
            held = []
        if middle is not None:
            held.append(middle)
        waiting = (prob, values) if prob is not None else None
        ready = scores

    gate_row = jnp.broadcast_to(jnp.sum(gate_row, axis=1, keepdims=True), (1, HD))
    gate_row += gate_in[0:1]
    gate_out[...] = jnp.broadcast_to(gate_row, gate_out.shape)
    code = coded(gate_row, CODE, rounded_here)
    rows = out_ref.shape[0] // 4
    for a, out in enumerate(out_refs):
        out[:rows] = out_ref[a * rows : (a + 1) * rows]
        for h in range(heads):
            out[rows:, h * HD : (h + 1) * HD] = code


def attention(at, sizes, gate_value, gate_in, columns, shared):
    n, n_blocks, n_images, heads, total_kv, tokens = sizes
    lead = at == 0
    read_most = n_images // 2
    img_tok = columns[0].shape[1] // 2
    queries = shared[2]
    groups = queries.shape[1] // HD // total_kv
    per_head = groups * n_blocks
    n_keys = read_most * img_tok
    smem = pl.BlockSpec(memory_space=pltpu.SMEM)
    vmem = pl.BlockSpec(memory_space=pltpu.VMEM)
    span = heads * HD
    args = [gate_value, gate_in, *columns]
    in_specs = [smem] + [vmem] * (1 + len(columns))
    args += shared
    in_specs += [smem, smem, vmem, vmem]
    out_shape = [
        pltpu.VMEM((heads, per_head, n_keys, BLK), BF16),
        pltpu.VMEM((heads, n_keys, HD), BF16),
        *[pltpu.VMEM((2 * n * img_tok + CODE, span), BF16)] * 4,
        pltpu.VMEM((8, HD), F32),
    ]
    rows = tokens * groups * heads
    kernel = functools.partial(
        attention_kernel, n, n_blocks, n_images, lead, at * heads, heads, total_kv, len(columns)
    )
    return pl.pallas_call(
        kernel,
        in_specs=in_specs,
        out_specs=[vmem] * len(out_shape),
        out_shape=out_shape,
        scratch_shapes=[
            pltpu.VMEM((4 * 2 * n * img_tok, span), BF16),
            pltpu.VMEM((heads, 4 * n, img_tok, HD), BF16),
            pltpu.VMEM((heads, 4 * n, img_tok, HD), BF16),
            pltpu.VMEM((heads, n_keys, HD), BF16),
            pltpu.VMEM((heads, n_keys, HD), F32),
            pltpu.VMEM((heads, n_keys, HD), F32),
        ],
        compiler_params=pltpu.CompilerParams(vmem_limit_bytes=vmem_bytes(n_keys)),
        cost_estimate=pl.CostEstimate(
            flops=8 * rows * n_keys * HD,
            bytes_accessed=4 * rows * HD,
            transcendentals=rows * n_keys,
        ),
        name="attention_backward",
    )(*args)


def vmem_bytes(n_keys):
    return min(44, 14 + 15 * n_keys // 1024) * 1024 * 1024


def query_kernel(first, n_blocks, n_extra, gate_ref, ds_ref, k_ref, *rest):
    dq_hbm, dq_ref, sem = rest[n_extra:]
    heads, per_head = ds_ref.shape[:2]
    groups = per_head // n_blocks
    width = groups * HD
    scale = gate_ref[0] * (1.0 / math.sqrt(HD))
    copies = []
    for h in range(heads):
        turned = k_ref[h].astype(F32).T.astype(BF16)
        for i in range(0, per_head, JOIN):
            b, g = i // groups, i % groups
            score_grad = jnp.concatenate([ds_ref[h, i + u] for u in range(JOIN)], axis=1)
            dq = jnp.dot(turned, score_grad, preferred_element_type=F32)
            dq = (dq.T * scale).astype(BF16)
            for u in range(JOIN):
                lanes = slice((g + u) * HD, (g + u + 1) * HD)
                dq_ref[h, b * BLK : (b + 1) * BLK, lanes] = dq[u * BLK : (u + 1) * BLK]
        span = pl.ds((first + h) * width, width)
        copies.append(pltpu.make_async_copy(dq_ref.at[h], dq_hbm.at[:, span], sem.at[h]))
        copies[-1].start()
    for copy in copies:
        copy.wait()


def query_gradient(at, sizes, shape, prev, after, gate_value, ds, kt):
    n, n_blocks, n_images, heads, total_kv, tokens = sizes
    hbm = pl.BlockSpec(memory_space=pltpu.HBM)
    vmem = pl.BlockSpec(memory_space=pltpu.VMEM)
    anywhere = pl.BlockSpec(memory_space=pl.ANY)
    extra = ([] if prev is None else [prev]) + after
    specs = ([] if prev is None else [hbm]) + [anywhere] * len(after)
    return pl.pallas_call(
        functools.partial(query_kernel, at * heads, n_blocks, len(extra)),
        in_specs=[pl.BlockSpec(memory_space=pltpu.SMEM), vmem, vmem] + specs,
        out_specs=hbm,
        out_shape=pltpu.HBM(shape, BF16),
        input_output_aliases={} if prev is None else {3: 0},
        scratch_shapes=[
            pltpu.VMEM((heads, shape[0], shape[1] // total_kv), BF16),
            pltpu.SemaphoreType.DMA((heads,)),
        ],
        compiler_params=pltpu.CompilerParams(vmem_limit_bytes=16 * 1024 * 1024),
        cost_estimate=pl.CostEstimate(
            flops=2 * ds.size * HD, bytes_accessed=2 * ds.size, transcendentals=0
        ),
        name="query_gradient",
    )(gate_value, ds, kt, *extra)


def per_device(queries, cotangent, image_keys, image_values, attn_gate, block_mask, image_owner):
    n_ctx = lax.axis_size("ctx")
    n_tp = lax.axis_size("tp")
    n = n_ctx // 4
    img_tok = image_keys.shape[1]
    local_kv = image_keys.shape[2] // HD
    chunks = min(CHUNKS, local_kv)
    heads = local_kv // chunks
    me = lax.axis_index("ctx").astype(jnp.int32).reshape(1)
    plan = jnp.concatenate([block_mask.reshape(-1), image_owner, me])
    gate_value = jnp.tanh(attn_gate)

    def swap(value, bit):
        return lax.ppermute(value, "ctx", [(i, i ^ bit) for i in range(n_ctx)])

    def swap_z(value, bit):
        pairs = [(i, (i // 4 ^ bit) * 4 + i % 4) for i in range(n_ctx)]
        return lax.ppermute(value, "ctx", pairs)

    def own_columns(c):
        lanes = slice(c * heads * HD, (c + 1) * heads * HD)
        return jnp.concatenate([image_keys[0, :, lanes], image_values[0, :, lanes]], axis=0)

    def square_of(own):
        pair = jnp.stack([own, swap(own, 1)])
        return jnp.concatenate([pair, swap(pair, 2)])

    def column_of(own):
        near_z.extend(swap_z(own, k) for k in range(1, n))
        return jnp.stack([own, *near_z])

    rest = 2 * n * img_tok

    def square_sum(own, came):
        total = own[:rest].astype(F32)
        gate = decoded(own[rest:])
        for part in came:
            total = total + part[:rest].astype(F32)
            gate = gate + decoded(part[rest:])
        return total.reshape(n, 2 * img_tok, own.shape[1]), gate

    def column_sum(both, gate, last):
        total, gate_total, turns = both[0], gate, []
        sends = both.astype(BF16)
        for k in range(1, n):
            send = sends[k]
            if last:
                send = jnp.concatenate([send, coded(gate, CODE, rounded_outside)])
            came = swap_z(send, k)
            turns.append(came)
            total = total + came[: 2 * img_tok].astype(F32)
            if last:
                gate_total = gate_total + decoded(came[2 * img_tok :])
        return total, gate_total, turns

    near_z = []
    owns = [own_columns(c) for c in range(chunks)]
    starts = [square_of(own) if c else column_of(own) for c, own in enumerate(owns)]
    sizes = (n, *block_mask.shape, heads, local_kv, queries.shape[0])
    shared = prepare(sizes, img_tok, plan, queries, cotangent, near_z[0])
    shared, starts = lax.optimization_barrier((tuple(shared), starts))
    column = starts[0]
    gathered = [[column, swap(column, 1), swap(column, 2), swap(column, 3)]]
    for square in starts[1:]:
        far = [swap_z(square, k) for k in range(2, n)]
        gathered[0][1], near = lax.optimization_barrier((gathered[0][1], square))
        gathered.append([square, swap_z(near, 1)] + far)
    gate_part = jnp.zeros((8, HD), F32)
    parts, dq = [], None
    saved, waiting = [], None
    for c in range(chunks):
        last = c == chunks - 1
        outs = attention(c, sizes, gate_value, gate_part, gathered[c], shared)
        ds, k_read, own, *backs, gate_part = outs
        if c:
            held = lax.optimization_barrier((tuple(backs), waiting[1]))
            backs = held[0]
            total, gate_row, turns = column_sum(*square_sum(waiting[0], held[1]), False)
            parts.append(total.astype(BF16))
        came = [swap(back, a + 1) for a, back in enumerate(backs)]
        waiting = (own, tuple(came))
        saved.append((ds, k_read))
    for c, (ds, k_read) in enumerate(saved):
        after = came[FIRST] if c == chunks - 1 else turns[0]
        dq = query_gradient(c, sizes, queries.shape, dq, [after], gate_value, ds, k_read)
    *came, dq = lax.optimization_barrier((*came, dq))
    total, gate_row, turns = column_sum(*square_sum(own, came), True)
    parts.append(total.astype(BF16))
    grads = jnp.concatenate(parts, axis=1)
    key_grad, value_grad = grads[None, :img_tok], grads[None, img_tok:]
    gate_total = gate_row
    for k in range(1, n_tp):
        pairs = [(i, (i + k) % n_tp) for i in range(n_tp)]
        gate_total = gate_total + lax.ppermute(gate_row, "tp", pairs)
    term_count = queries.shape[0] * n_ctx * queries.shape[1] * n_tp
    gate_row = gate_total[0, :HD] * (1.0 / math.sqrt(term_count))
    gate_grad = ((1.0 - gate_value * gate_value) * gate_row)[:1]
    return (dq, key_grad, value_grad, gate_grad)


def solution(mesh):
    in_specs = (
        P("ctx", "tp"),
        P("ctx", "tp"),
        P("ctx", None, "tp"),
        P("ctx", None, "tp"),
        P(),
        P("ctx", None),
        P(),
    )
    out_specs = (P("ctx", "tp"), P("ctx", None, "tp"), P("ctx", None, "tp"), P())
    return jax.shard_map(
        per_device, mesh=mesh, in_specs=in_specs, out_specs=out_specs, check_vma=False
    )
```

```python
import functools
import math

import jax
import jax.numpy as jnp
from jax import lax
from jax.experimental import pallas as pl
from jax.experimental.pallas import tpu as pltpu
from jax.sharding import PartitionSpec as P

HD = 128
BLK = 128
JOIN = 4
FIRST = 0
MERGE = 2
CHUNKS = 2
CODE = 16
NT = (((1,), (1,)), ((), ()))
F32, BF16 = jnp.float32, jnp.bfloat16


def coded(value, rows, rounded):
    high = rounded(value)
    middle = rounded(value - high)
    low = value - high - middle
    shape = (rows, value.shape[1])
    row = lax.broadcasted_iota(jnp.int32, shape, 0)
    parts = jnp.where(row == 0, high, jnp.zeros(shape, F32))
    return jnp.where(row == 1, middle, jnp.where(row == 2, low, parts)).astype(BF16)


def rounded_here(value):
    return value.astype(BF16).astype(F32)


def rounded_outside(value):
    return lax.reduce_precision(value, 8, 7)


def decoded(rows):
    rows = rows.astype(F32)
    return rows[0:1] + rows[1:2] + rows[2:3]


def plan_images(n, n_blocks, n_images, part_rows, plan_ref, place, bias):
    read_most = n_images // 2
    me = plan_ref[(n_blocks + 1) * n_images]
    for j in range(read_most):
        place[0, j] = 0
        place[1, j] = 0
        place[2, j] = 0
        for b in range(n_blocks):
            bias[b, j] = jnp.float32(-1e30)

    def look(i, count):
        reads = [plan_ref[b * n_images + i] > 0 for b in range(n_blocks)]
        any_read = functools.reduce(jnp.logical_or, reads)

        @pl.when(jnp.logical_and(any_read, count < read_most))
        def _():
            slot = plan_ref[n_blocks * n_images + i]
            column = jnp.bitwise_xor(lax.rem(slot, 4), lax.rem(me, 4))
            across = jnp.bitwise_xor(lax.div(slot, 4), lax.div(me, 4))
            place[0, count] = column * n + across
            place[1, count] = across * 4 + column
            place[2, count] = (column * n + across) * part_rows
            for b in range(n_blocks):
                bias[b, count] = jnp.where(reads[b], 0.0, -1e30).astype(F32)

        return count + any_read.astype(jnp.int32)

    lax.fori_loop(0, n_images, look, jnp.int32(0))


def prepare_kernel(n, n_blocks, n_images, part_rows, *refs):
    plan_ref, q_hbm, cot_hbm, _, place, bias, q_ref, cot_ref, sem = refs
    half = q_ref.shape[0] // 2
    copies = []
    for u, (src, dst) in enumerate(((q_hbm, q_ref), (cot_hbm, cot_ref))):
        for k in range(2):
            rows = slice(k * half, (k + 1) * half)
            copies.append(pltpu.make_async_copy(src.at[rows], dst.at[rows], sem.at[u, k]))
            copies[-1].start()
    plan_images(n, n_blocks, n_images, part_rows, plan_ref, place, bias)
    for copy in copies:
        copy.wait()


def prepare(sizes, img_tok, plan, queries, cotangent, after):
    n, n_blocks, n_images = sizes[:3]
    smem = pl.BlockSpec(memory_space=pltpu.SMEM)
    vmem = pl.BlockSpec(memory_space=pltpu.VMEM)
    hbm = pl.BlockSpec(memory_space=pltpu.HBM)
    wide = [pltpu.with_memory_space_constraint(x, pltpu.HBM) for x in (queries, cotangent)]
    return pl.pallas_call(
        functools.partial(prepare_kernel, n, n_blocks, n_images, 2 * img_tok),
        in_specs=[smem, hbm, hbm, pl.BlockSpec(memory_space=pl.ANY)],
        out_specs=[smem, smem, vmem, vmem],
        out_shape=[
            jax.ShapeDtypeStruct((3, n_images // 2), jnp.int32),
            jax.ShapeDtypeStruct((n_blocks, n_images // 2), F32),
            pltpu.VMEM(queries.shape, BF16),
            pltpu.VMEM(queries.shape, BF16),
        ],
        scratch_shapes=[pltpu.SemaphoreType.DMA((2, 2))],
        compiler_params=pltpu.CompilerParams(vmem_limit_bytes=4 * 1024 * 1024),
        cost_estimate=pl.CostEstimate(
            flops=0, bytes_accessed=8 * queries.size, transcendentals=0
        ),
        name="prepare",
    )(plan, *wide, after)


def attention_kernel(n, n_blocks, n_images, lead, first, heads, total_kv, n_columns, *refs):
    gate_ref, gate_in = refs[:2]
    columns = refs[2 : 2 + n_columns]
    refs = refs[2 + n_columns :]
    place, bias, q_ref, cot_ref = refs[:4]
    ds_ref, k_sel = refs[4:6]
    out_refs = refs[6:10]
    gate_out, out_ref, k_all, v_all, v_sel, dk_acc, dv_acc = refs[10:]
    read_most = n_images // 2
    img_tok = k_all.shape[2]
    per_head = ds_ref.shape[1]
    groups = per_head // n_blocks
    width = groups * HD
    gate_value = gate_ref[0]
    inv_root = 1.0 / math.sqrt(HD)
    to_exp2 = math.log2(math.e) * inv_root

    for h in range(heads):
        lanes = slice(h * HD, (h + 1) * HD)
        at = 0
        for column in columns:
            count = column.shape[0]
            k_all[h, at : at + count] = column[:, :img_tok, lanes]
            v_all[h, at : at + count] = column[:, img_tok:, lanes]
            at += count
        for j in range(read_most):
            rows = slice(j * img_tok, (j + 1) * img_tok)
            where = place[0 if lead else 1, j]
            k_sel[h, rows] = k_all[h, where]
            v_sel[h, rows] = v_all[h, where]
    out_ref[...] = jnp.zeros_like(out_ref)
    dk_acc[...] = jnp.zeros_like(dk_acc)
    dv_acc[...] = jnp.zeros_like(dv_acc)

    def tile_of(ref, i):
        h, b, g = i // per_head, i % per_head // groups, i % groups
        lane = ((first + h) * groups + g) * HD
        return ref[b * BLK : (b + 1) * BLK, lane : lane + HD]

    def score_product(i):
        h = i // per_head
        return lax.dot_general(k_sel[h], tile_of(q_ref, i), NT, preferred_element_type=F32)

    def value_product(i):
        h = i // per_head
        return lax.dot_general(v_sel[h], tile_of(cot_ref, i), NT, preferred_element_type=F32)

    def probabilities(i, scores):
        b = i % per_head // groups
        images = [scores[j * img_tok : (j + 1) * img_tok] for j in range(read_most)]
        tops = [
            jnp.max(image.reshape(img_tok // 8, 8, BLK), axis=0) + bias[b, j]
            for j, image in enumerate(images)
        ]
        row_max = jnp.max(functools.reduce(jnp.maximum, tops), axis=0, keepdims=True)
        terms = [
            jnp.exp2((image - (row_max - bias[b, j])) * to_exp2) for j, image in enumerate(images)
        ]
        terms = jnp.concatenate(terms, axis=0)
        return terms * (1.0 / jnp.sum(terms, axis=0, keepdims=True))

    def score_gradient(i, prob, prob_grad):
        delta = jnp.sum(prob * prob_grad, axis=0, keepdims=True)
        score_grad = (prob * (prob_grad - delta)).astype(BF16)
        ds_ref[i // per_head, i % per_head] = score_grad
        return prob.astype(BF16), score_grad

    def gradients(pieces):
        h = pieces[0][0] // per_head
        query = jnp.concatenate([tile_of(q_ref, i) for i, _, _ in pieces], axis=0)
        cot = jnp.concatenate([tile_of(cot_ref, i) for i, _, _ in pieces], axis=0)
        prob_half = jnp.concatenate([p for _, p, _ in pieces], axis=1)
        score_grad = jnp.concatenate([d for _, _, d in pieces], axis=1)
        dk_acc[h] += jnp.dot(score_grad, query, preferred_element_type=F32)
        dv_acc[h] += jnp.dot(prob_half, cot, preferred_element_type=F32)

    def finish(h):
        lanes = slice(h * HD, (h + 1) * HD)
        for j in range(read_most):
            rows = slice(j * img_tok, (j + 1) * img_tok)
            at = place[2, j]
            for u, (acc, scale) in enumerate(((dk_acc, gate_value * inv_root), (dv_acc, gate_value))):
                out_rows = pl.ds(pl.multiple_of(at + u * img_tok, 16), img_tok)
                out_ref[out_rows, lanes] = (acc[h, rows] * scale).astype(BF16)
        return jnp.sum(dv_acc[h] * v_sel[h].astype(F32), axis=0, keepdims=True)

    items = heads * per_head
    gate_row = jnp.zeros((1, HD), F32)
    ready, waiting, held = None, None, []
    for at in range(items + 3):
        scores = score_product(at) if at < items else None
        values = value_product(at - 1) if 0 < at <= items else None
        prob = probabilities(at - 1, ready) if ready is not None else None
        middle = (at - 2, *score_gradient(at - 2, *waiting)) if waiting is not None else None
        if len(held) == MERGE:
            gradients(held)
            if (held[-1][0] + 1) % per_head == 0:
                gate_row += finish(held[-1][0] // per_head)
            held = []
        if middle is not None:
            held.append(middle)
        waiting = (prob, values) if prob is not None else None
        ready = scores

    gate_row = jnp.broadcast_to(jnp.sum(gate_row, axis=1, keepdims=True), (1, HD))
    gate_row += gate_in[0:1]
    gate_out[...] = jnp.broadcast_to(gate_row, gate_out.shape)
    code = coded(gate_row, CODE, rounded_here)
    rows = out_ref.shape[0] // 4
    for a, out in enumerate(out_refs):
        out[:rows] = out_ref[a * rows : (a + 1) * rows]
        for h in range(heads):
            out[rows:, h * HD : (h + 1) * HD] = code


def attention(at, sizes, gate_value, gate_in, columns, shared):
    n, n_blocks, n_images, heads, total_kv, tokens = sizes
    lead = at == 0
    read_most = n_images // 2
    img_tok = columns[0].shape[1] // 2
    queries = shared[2]
    groups = queries.shape[1] // HD // total_kv
    per_head = groups * n_blocks
    n_keys = read_most * img_tok
    smem = pl.BlockSpec(memory_space=pltpu.SMEM)
    vmem = pl.BlockSpec(memory_space=pltpu.VMEM)
    span = heads * HD
    args = [gate_value, gate_in, *columns]
    in_specs = [smem] + [vmem] * (1 + len(columns))
    args += shared
    in_specs += [smem, smem, vmem, vmem]
    out_shape = [
        pltpu.VMEM((heads, per_head, n_keys, BLK), BF16),
        pltpu.VMEM((heads, n_keys, HD), BF16),
        *[pltpu.VMEM((2 * n * img_tok + CODE, span), BF16)] * 4,
        pltpu.VMEM((8, HD), F32),
    ]
    rows = tokens * groups * heads
    kernel = functools.partial(
        attention_kernel, n, n_blocks, n_images, lead, at * heads, heads, total_kv, len(columns)
    )
    return pl.pallas_call(
        kernel,
        in_specs=in_specs,
        out_specs=[vmem] * len(out_shape),
        out_shape=out_shape,
        scratch_shapes=[
            pltpu.VMEM((4 * 2 * n * img_tok, span), BF16),
            pltpu.VMEM((heads, 4 * n, img_tok, HD), BF16),
            pltpu.VMEM((heads, 4 * n, img_tok, HD), BF16),
            pltpu.VMEM((heads, n_keys, HD), BF16),
            pltpu.VMEM((heads, n_keys, HD), F32),
            pltpu.VMEM((heads, n_keys, HD), F32),
        ],
        compiler_params=pltpu.CompilerParams(vmem_limit_bytes=vmem_bytes(n_keys)),
        cost_estimate=pl.CostEstimate(
            flops=8 * rows * n_keys * HD,
            bytes_accessed=4 * rows * HD,
            transcendentals=rows * n_keys,
        ),
        name="attention_backward",
    )(*args)


def vmem_bytes(n_keys):
    return min(44, 14 + 15 * n_keys // 1024) * 1024 * 1024


def query_kernel(first, n_blocks, n_extra, gate_ref, ds_ref, k_ref, *rest):
    dq_hbm, dq_ref, sem = rest[n_extra:]
    heads, per_head = ds_ref.shape[:2]
    groups = per_head // n_blocks
    width = groups * HD
    scale = gate_ref[0] * (1.0 / math.sqrt(HD))
    copies = []
    for h in range(heads):
        turned = k_ref[h].astype(F32).T.astype(BF16)
        for i in range(0, per_head, JOIN):
            b, g = i // groups, i % groups
            score_grad = jnp.concatenate([ds_ref[h, i + u] for u in range(JOIN)], axis=1)
            dq = jnp.dot(turned, score_grad, preferred_element_type=F32)
            dq = (dq.T * scale).astype(BF16)
            for u in range(JOIN):
                lanes = slice((g + u) * HD, (g + u + 1) * HD)
                dq_ref[h, b * BLK : (b + 1) * BLK, lanes] = dq[u * BLK : (u + 1) * BLK]
        span = pl.ds((first + h) * width, width)
        copies.append(pltpu.make_async_copy(dq_ref.at[h], dq_hbm.at[:, span], sem.at[h]))
        copies[-1].start()
    for copy in copies:
        copy.wait()


def query_gradient(at, sizes, shape, prev, after, gate_value, ds, kt):
    n, n_blocks, n_images, heads, total_kv, tokens = sizes
    hbm = pl.BlockSpec(memory_space=pltpu.HBM)
    vmem = pl.BlockSpec(memory_space=pltpu.VMEM)
    anywhere = pl.BlockSpec(memory_space=pl.ANY)
    extra = ([] if prev is None else [prev]) + after
    specs = ([] if prev is None else [hbm]) + [anywhere] * len(after)
    return pl.pallas_call(
        functools.partial(query_kernel, at * heads, n_blocks, len(extra)),
        in_specs=[pl.BlockSpec(memory_space=pltpu.SMEM), vmem, vmem] + specs,
        out_specs=hbm,
        out_shape=pltpu.HBM(shape, BF16),
        input_output_aliases={} if prev is None else {3: 0},
        scratch_shapes=[
            pltpu.VMEM((heads, shape[0], shape[1] // total_kv), BF16),
            pltpu.SemaphoreType.DMA((heads,)),
        ],
        compiler_params=pltpu.CompilerParams(vmem_limit_bytes=16 * 1024 * 1024),
        cost_estimate=pl.CostEstimate(
            flops=2 * ds.size * HD, bytes_accessed=2 * ds.size, transcendentals=0
        ),
        name="query_gradient",
    )(gate_value, ds, kt, *extra)


def per_device(queries, cotangent, image_keys, image_values, attn_gate, block_mask, image_owner):
    n_ctx = lax.axis_size("ctx")
    n_tp = lax.axis_size("tp")
    n = n_ctx // 4
    img_tok = image_keys.shape[1]
    local_kv = image_keys.shape[2] // HD
    chunks = min(CHUNKS, local_kv)
    heads = local_kv // chunks
    me = lax.axis_index("ctx").astype(jnp.int32).reshape(1)
    plan = jnp.concatenate([block_mask.reshape(-1), image_owner, me])
    gate_value = jnp.tanh(attn_gate)

    def swap(value, bit):
        return lax.ppermute(value, "ctx", [(i, i ^ bit) for i in range(n_ctx)])

    def swap_z(value, bit):
        pairs = [(i, (i // 4 ^ bit) * 4 + i % 4) for i in range(n_ctx)]
        return lax.ppermute(value, "ctx", pairs)

    def own_columns(c):
        lanes = slice(c * heads * HD, (c + 1) * heads * HD)
        return jnp.concatenate([image_keys[0, :, lanes], image_values[0, :, lanes]], axis=0)

    def square_of(own):
        pair = jnp.stack([own, swap(own, 1)])
        return jnp.concatenate([pair, swap(pair, 2)])

    def column_of(own):
        near_z.extend(swap_z(own, k) for k in range(1, n))
        return jnp.stack([own, *near_z])

    rest = 2 * n * img_tok

    def square_sum(own, came):
        total = own[:rest].astype(F32)
        gate = decoded(own[rest:])
        for part in came:
            total = total + part[:rest].astype(F32)
            gate = gate + decoded(part[rest:])
        return total.reshape(n, 2 * img_tok, own.shape[1]), gate

    def column_sum(both, gate, last):
        total, gate_total, turns = both[0], gate, []
        sends = both.astype(BF16)
        for k in range(1, n):
            send = sends[k]
            if last:
                send = jnp.concatenate([send, coded(gate, CODE, rounded_outside)])
            came = swap_z(send, k)
            turns.append(came)
            total = total + came[: 2 * img_tok].astype(F32)
            if last:
                gate_total = gate_total + decoded(came[2 * img_tok :])
        return total, gate_total, turns

    near_z = []
    owns = [own_columns(c) for c in range(chunks)]
    starts = [square_of(own) if c else column_of(own) for c, own in enumerate(owns)]
    sizes = (n, *block_mask.shape, heads, local_kv, queries.shape[0])
    plan, starts, gate_value = lax.optimization_barrier((plan, starts, gate_value))
    column = starts[0]
    gathered = [[column, swap(column, 1), swap(column, 2), swap(column, 3)]]
    shared = tuple(prepare(sizes, img_tok, plan, queries, cotangent, gathered[0][1]))
    for square in starts[1:]:
        far = [swap_z(square, k) for k in range(2, n)]
        gathered[0][1], near = lax.optimization_barrier((gathered[0][1], square))
        gathered.append([square, swap_z(near, 1)] + far)
    gate_part = jnp.zeros((8, HD), F32)
    parts, dq = [], None
    saved, waiting = [], None
    for c in range(chunks):
        last = c == chunks - 1
        outs = attention(c, sizes, gate_value, gate_part, gathered[c], shared)
        ds, k_read, own, *backs, gate_part = outs
        if c:
            held = lax.optimization_barrier((tuple(backs), waiting[1]))
            backs = held[0]
            total, gate_row, turns = column_sum(*square_sum(waiting[0], held[1]), False)
            parts.append(total.astype(BF16))
        came = [swap(back, a + 1) for a, back in enumerate(backs)]
        waiting = (own, tuple(came))
        saved.append((ds, k_read))
    for c, (ds, k_read) in enumerate(saved):
        after = came[FIRST] if c == chunks - 1 else turns[0]
        dq = query_gradient(c, sizes, queries.shape, dq, [after], gate_value, ds, k_read)
    *came, dq = lax.optimization_barrier((*came, dq))
    total, gate_row, turns = column_sum(*square_sum(own, came), True)
    parts.append(total.astype(BF16))
    grads = jnp.concatenate(parts, axis=1)
    key_grad, value_grad = grads[None, :img_tok], grads[None, img_tok:]
    gate_total = gate_row
    for k in range(1, n_tp):
        pairs = [(i, (i + k) % n_tp) for i in range(n_tp)]
        gate_total = gate_total + lax.ppermute(gate_row, "tp", pairs)
    term_count = queries.shape[0] * n_ctx * queries.shape[1] * n_tp
    gate_row = gate_total[0, :HD] * (1.0 / math.sqrt(term_count))
    gate_grad = ((1.0 - gate_value * gate_value) * gate_row)[:1]
    return (dq, key_grad, value_grad, gate_grad)


def solution(mesh):
    in_specs = (
        P("ctx", "tp"),
        P("ctx", "tp"),
        P("ctx", None, "tp"),
        P("ctx", None, "tp"),
        P(),
        P("ctx", None),
        P(),
    )
    out_specs = (P("ctx", "tp"), P("ctx", None, "tp"), P("ctx", None, "tp"), P())
    return jax.shard_map(
        per_device, mesh=mesh, in_specs=in_specs, out_specs=out_specs, check_vma=False
    )
```

```python
import functools
import math

import jax
import jax.numpy as jnp
from jax import lax
from jax.experimental import pallas as pl
from jax.experimental.pallas import tpu as pltpu
from jax.sharding import PartitionSpec as P

HD = 128
BLK = 128
JOIN = 4
FIRST = 0
MERGE = 2
CHUNKS = 2
CODE = 16
NT = (((1,), (1,)), ((), ()))
F32, BF16 = jnp.float32, jnp.bfloat16


def coded(value, rows, rounded):
    high = rounded(value)
    middle = rounded(value - high)
    low = value - high - middle
    shape = (rows, value.shape[1])
    row = lax.broadcasted_iota(jnp.int32, shape, 0)
    parts = jnp.where(row == 0, high, jnp.zeros(shape, F32))
    return jnp.where(row == 1, middle, jnp.where(row == 2, low, parts)).astype(BF16)


def rounded_here(value):
    return value.astype(BF16).astype(F32)


def rounded_outside(value):
    return lax.reduce_precision(value, 8, 7)


def decoded(rows):
    rows = rows.astype(F32)
    return rows[0:1] + rows[1:2] + rows[2:3]


def plan_images(n, n_blocks, n_images, part_rows, plan_ref, place, bias):
    read_most = n_images // 2
    me = plan_ref[(n_blocks + 1) * n_images]
    for j in range(read_most):
        place[0, j] = 0
        place[1, j] = 0
        place[2, j] = 0
        for b in range(n_blocks):
            bias[b, j] = jnp.float32(-1e30)

    def look(i, count):
        reads = [plan_ref[b * n_images + i] > 0 for b in range(n_blocks)]
        any_read = functools.reduce(jnp.logical_or, reads)

        @pl.when(jnp.logical_and(any_read, count < read_most))
        def _():
            slot = plan_ref[n_blocks * n_images + i]
            column = jnp.bitwise_xor(lax.rem(slot, 4), lax.rem(me, 4))
            across = jnp.bitwise_xor(lax.div(slot, 4), lax.div(me, 4))
            place[0, count] = column * n + across
            place[1, count] = across * 4 + column
            place[2, count] = (column * n + across) * part_rows
            for b in range(n_blocks):
                bias[b, count] = jnp.where(reads[b], 0.0, -1e30).astype(F32)

        return count + any_read.astype(jnp.int32)

    lax.fori_loop(0, n_images, look, jnp.int32(0))


def prepare_kernel(n, n_blocks, n_images, part_rows, *refs):
    plan_ref, q_hbm, cot_hbm, _, place, bias, q_ref, cot_ref, sem = refs
    half = q_ref.shape[0] // 2
    copies = []
    for u, (src, dst) in enumerate(((q_hbm, q_ref), (cot_hbm, cot_ref))):
        for k in range(2):
            rows = slice(k * half, (k + 1) * half)
            copies.append(pltpu.make_async_copy(src.at[rows], dst.at[rows], sem.at[u, k]))
            copies[-1].start()
    plan_images(n, n_blocks, n_images, part_rows, plan_ref, place, bias)
    for copy in copies:
        copy.wait()


def prepare(sizes, img_tok, plan, queries, cotangent, after):
    n, n_blocks, n_images = sizes[:3]
    smem = pl.BlockSpec(memory_space=pltpu.SMEM)
    vmem = pl.BlockSpec(memory_space=pltpu.VMEM)
    hbm = pl.BlockSpec(memory_space=pltpu.HBM)
    wide = [pltpu.with_memory_space_constraint(x, pltpu.HBM) for x in (queries, cotangent)]
    return pl.pallas_call(
        functools.partial(prepare_kernel, n, n_blocks, n_images, 2 * img_tok),
        in_specs=[smem, hbm, hbm, pl.BlockSpec(memory_space=pl.ANY)],
        out_specs=[smem, smem, vmem, vmem],
        out_shape=[
            jax.ShapeDtypeStruct((3, n_images // 2), jnp.int32),
            jax.ShapeDtypeStruct((n_blocks, n_images // 2), F32),
            pltpu.VMEM(queries.shape, BF16),
            pltpu.VMEM(queries.shape, BF16),
        ],
        scratch_shapes=[pltpu.SemaphoreType.DMA((2, 2))],
        compiler_params=pltpu.CompilerParams(vmem_limit_bytes=4 * 1024 * 1024),
        cost_estimate=pl.CostEstimate(
            flops=0, bytes_accessed=8 * queries.size, transcendentals=0
        ),
        name="prepare",
    )(plan, *wide, after)


def attention_kernel(n, n_blocks, n_images, lead, first, heads, total_kv, n_columns, *refs):
    gate_ref, gate_in = refs[:2]
    columns = refs[2 : 2 + n_columns]
    refs = refs[2 + n_columns :]
    place, bias, q_ref, cot_ref = refs[:4]
    ds_ref, k_sel = refs[4:6]
    out_refs = refs[6:10]
    gate_out, out_ref, k_all, v_all, v_sel, dk_acc, dv_acc = refs[10:]
    read_most = n_images // 2
    img_tok = k_all.shape[2]
    per_head = ds_ref.shape[1]
    groups = per_head // n_blocks
    width = groups * HD
    gate_value = gate_ref[0]
    inv_root = 1.0 / math.sqrt(HD)
    to_exp2 = math.log2(math.e) * inv_root

    for h in range(heads):
        lanes = slice(h * HD, (h + 1) * HD)
        at = 0
        for column in columns:
            count = column.shape[0]
            k_all[h, at : at + count] = column[:, :img_tok, lanes]
            v_all[h, at : at + count] = column[:, img_tok:, lanes]
            at += count
        for j in range(read_most):
            rows = slice(j * img_tok, (j + 1) * img_tok)
            where = place[0 if lead else 1, j]
            k_sel[h, rows] = k_all[h, where]
            v_sel[h, rows] = v_all[h, where]
    out_ref[...] = jnp.zeros_like(out_ref)
    dk_acc[...] = jnp.zeros_like(dk_acc)
    dv_acc[...] = jnp.zeros_like(dv_acc)

    def tile_of(ref, i):
        h, b, g = i // per_head, i % per_head // groups, i % groups
        lane = ((first + h) * groups + g) * HD
        return ref[b * BLK : (b + 1) * BLK, lane : lane + HD]

    def score_product(i):
        h = i // per_head
        return lax.dot_general(k_sel[h], tile_of(q_ref, i), NT, preferred_element_type=F32)

    def value_product(i):
        h = i // per_head
        return lax.dot_general(v_sel[h], tile_of(cot_ref, i), NT, preferred_element_type=F32)

    def probabilities(i, scores):
        b = i % per_head // groups
        images = [scores[j * img_tok : (j + 1) * img_tok] for j in range(read_most)]
        tops = [
            jnp.max(image.reshape(img_tok // 8, 8, BLK), axis=0) + bias[b, j]
            for j, image in enumerate(images)
        ]
        row_max = jnp.max(functools.reduce(jnp.maximum, tops), axis=0, keepdims=True)
        terms = [
            jnp.exp2((image - (row_max - bias[b, j])) * to_exp2) for j, image in enumerate(images)
        ]
        terms = jnp.concatenate(terms, axis=0)
        return terms * (1.0 / jnp.sum(terms, axis=0, keepdims=True))

    def score_gradient(i, prob, prob_grad):
        delta = jnp.sum(prob * prob_grad, axis=0, keepdims=True)
        score_grad = (prob * (prob_grad - delta)).astype(BF16)
        ds_ref[i // per_head, i % per_head] = score_grad
        return prob.astype(BF16), score_grad

    def gradients(pieces):
        h = pieces[0][0] // per_head
        query = jnp.concatenate([tile_of(q_ref, i) for i, _, _ in pieces], axis=0)
        cot = jnp.concatenate([tile_of(cot_ref, i) for i, _, _ in pieces], axis=0)
        prob_half = jnp.concatenate([p for _, p, _ in pieces], axis=1)
        score_grad = jnp.concatenate([d for _, _, d in pieces], axis=1)
        dk_acc[h] += jnp.dot(score_grad, query, preferred_element_type=F32)
        dv_acc[h] += jnp.dot(prob_half, cot, preferred_element_type=F32)

    def finish(h):
        lanes = slice(h * HD, (h + 1) * HD)
        for j in range(read_most):
            rows = slice(j * img_tok, (j + 1) * img_tok)
            at = place[2, j]
            for u, (acc, scale) in enumerate(((dk_acc, gate_value * inv_root), (dv_acc, gate_value))):
                out_rows = pl.ds(pl.multiple_of(at + u * img_tok, 16), img_tok)
                out_ref[out_rows, lanes] = (acc[h, rows] * scale).astype(BF16)
        return jnp.sum(dv_acc[h] * v_sel[h].astype(F32), axis=0, keepdims=True)

    items = heads * per_head
    gate_row = jnp.zeros((1, HD), F32)
    ready, waiting, held = None, None, []
    for at in range(items + 3):
        scores = score_product(at) if at < items else None
        values = value_product(at - 1) if 0 < at <= items else None
        if len(held) == MERGE:
            gradients(held)
            if (held[-1][0] + 1) % per_head == 0:
                gate_row += finish(held[-1][0] // per_head)
            held = []
        prob = probabilities(at - 1, ready) if ready is not None else None
        middle = (at - 2, *score_gradient(at - 2, *waiting)) if waiting is not None else None
        if middle is not None:
            held.append(middle)
        waiting = (prob, values) if prob is not None else None
        ready = scores

    gate_row = jnp.broadcast_to(jnp.sum(gate_row, axis=1, keepdims=True), (1, HD))
    gate_row += gate_in[0:1]
    gate_out[...] = jnp.broadcast_to(gate_row, gate_out.shape)
    code = coded(gate_row, CODE, rounded_here)
    rows = out_ref.shape[0] // 4
    for a, out in enumerate(out_refs):
        out[:rows] = out_ref[a * rows : (a + 1) * rows]
        for h in range(heads):
            out[rows:, h * HD : (h + 1) * HD] = code


def attention(at, sizes, gate_value, gate_in, columns, shared):
    n, n_blocks, n_images, heads, total_kv, tokens = sizes
    lead = at == 0
    read_most = n_images // 2
    img_tok = columns[0].shape[1] // 2
    queries = shared[2]
    groups = queries.shape[1] // HD // total_kv
    per_head = groups * n_blocks
    n_keys = read_most * img_tok
    smem = pl.BlockSpec(memory_space=pltpu.SMEM)
    vmem = pl.BlockSpec(memory_space=pltpu.VMEM)
    span = heads * HD
    args = [gate_value, gate_in, *columns]
    in_specs = [smem] + [vmem] * (1 + len(columns))
    args += shared
    in_specs += [smem, smem, vmem, vmem]
    out_shape = [
        pltpu.VMEM((heads, per_head, n_keys, BLK), BF16),
        pltpu.VMEM((heads, n_keys, HD), BF16),
        *[pltpu.VMEM((2 * n * img_tok + CODE, span), BF16)] * 4,
        pltpu.VMEM((8, HD), F32),
    ]
    rows = tokens * groups * heads
    kernel = functools.partial(
        attention_kernel, n, n_blocks, n_images, lead, at * heads, heads, total_kv, len(columns)
    )
    return pl.pallas_call(
        kernel,
        in_specs=in_specs,
        out_specs=[vmem] * len(out_shape),
        out_shape=out_shape,
        scratch_shapes=[
            pltpu.VMEM((4 * 2 * n * img_tok, span), BF16),
            pltpu.VMEM((heads, 4 * n, img_tok, HD), BF16),
            pltpu.VMEM((heads, 4 * n, img_tok, HD), BF16),
            pltpu.VMEM((heads, n_keys, HD), BF16),
            pltpu.VMEM((heads, n_keys, HD), F32),
            pltpu.VMEM((heads, n_keys, HD), F32),
        ],
        compiler_params=pltpu.CompilerParams(vmem_limit_bytes=vmem_bytes(n_keys)),
        cost_estimate=pl.CostEstimate(
            flops=8 * rows * n_keys * HD,
            bytes_accessed=4 * rows * HD,
            transcendentals=rows * n_keys,
        ),
        name="attention_backward",
    )(*args)


def vmem_bytes(n_keys):
    return min(44, 14 + 15 * n_keys // 1024) * 1024 * 1024


def query_kernel(first, n_blocks, n_extra, gate_ref, ds_ref, k_ref, *rest):
    dq_hbm, dq_ref, sem = rest[n_extra:]
    heads, per_head = ds_ref.shape[:2]
    groups = per_head // n_blocks
    width = groups * HD
    scale = gate_ref[0] * (1.0 / math.sqrt(HD))
    copies = []
    for h in range(heads):
        turned = k_ref[h].astype(F32).T.astype(BF16)
        for i in range(0, per_head, JOIN):
            b, g = i // groups, i % groups
            score_grad = jnp.concatenate([ds_ref[h, i + u] for u in range(JOIN)], axis=1)
            dq = jnp.dot(turned, score_grad, preferred_element_type=F32)
            dq = (dq.T * scale).astype(BF16)
            for u in range(JOIN):
                lanes = slice((g + u) * HD, (g + u + 1) * HD)
                dq_ref[h, b * BLK : (b + 1) * BLK, lanes] = dq[u * BLK : (u + 1) * BLK]
        span = pl.ds((first + h) * width, width)
        copies.append(pltpu.make_async_copy(dq_ref.at[h], dq_hbm.at[:, span], sem.at[h]))
        copies[-1].start()
    for copy in copies:
        copy.wait()


def query_gradient(at, sizes, shape, prev, after, gate_value, ds, kt):
    n, n_blocks, n_images, heads, total_kv, tokens = sizes
    hbm = pl.BlockSpec(memory_space=pltpu.HBM)
    vmem = pl.BlockSpec(memory_space=pltpu.VMEM)
    anywhere = pl.BlockSpec(memory_space=pl.ANY)
    extra = ([] if prev is None else [prev]) + after
    specs = ([] if prev is None else [hbm]) + [anywhere] * len(after)
    return pl.pallas_call(
        functools.partial(query_kernel, at * heads, n_blocks, len(extra)),
        in_specs=[pl.BlockSpec(memory_space=pltpu.SMEM), vmem, vmem] + specs,
        out_specs=hbm,
        out_shape=pltpu.HBM(shape, BF16),
        input_output_aliases={} if prev is None else {3: 0},
        scratch_shapes=[
            pltpu.VMEM((heads, shape[0], shape[1] // total_kv), BF16),
            pltpu.SemaphoreType.DMA((heads,)),
        ],
        compiler_params=pltpu.CompilerParams(vmem_limit_bytes=16 * 1024 * 1024),
        cost_estimate=pl.CostEstimate(
            flops=2 * ds.size * HD, bytes_accessed=2 * ds.size, transcendentals=0
        ),
        name="query_gradient",
    )(gate_value, ds, kt, *extra)


def per_device(queries, cotangent, image_keys, image_values, attn_gate, block_mask, image_owner):
    n_ctx = lax.axis_size("ctx")
    n_tp = lax.axis_size("tp")
    n = n_ctx // 4
    img_tok = image_keys.shape[1]
    local_kv = image_keys.shape[2] // HD
    chunks = min(CHUNKS, local_kv)
    heads = local_kv // chunks
    me = lax.axis_index("ctx").astype(jnp.int32).reshape(1)
    plan = jnp.concatenate([block_mask.reshape(-1), image_owner, me])
    gate_value = jnp.tanh(attn_gate)

    def swap(value, bit):
        return lax.ppermute(value, "ctx", [(i, i ^ bit) for i in range(n_ctx)])

    def swap_z(value, bit):
        pairs = [(i, (i // 4 ^ bit) * 4 + i % 4) for i in range(n_ctx)]
        return lax.ppermute(value, "ctx", pairs)

    def own_columns(c):
        lanes = slice(c * heads * HD, (c + 1) * heads * HD)
        return jnp.concatenate([image_keys[0, :, lanes], image_values[0, :, lanes]], axis=0)

    def square_of(own):
        pair = jnp.stack([own, swap(own, 1)])
        return jnp.concatenate([pair, swap(pair, 2)])

    def column_of(own):
        near_z.extend(swap_z(own, k) for k in range(1, n))
        return jnp.stack([own, *near_z])

    rest = 2 * n * img_tok

    def square_sum(own, came):
        total = own[:rest].astype(F32)
        gate = decoded(own[rest:])
        for part in came:
            total = total + part[:rest].astype(F32)
            gate = gate + decoded(part[rest:])
        return total.reshape(n, 2 * img_tok, own.shape[1]), gate

    def column_sum(both, gate, last):
        total, gate_total, turns = both[0], gate, []
        sends = both.astype(BF16)
        for k in range(1, n):
            send = sends[k]
            if last:
                send = jnp.concatenate([send, coded(gate, CODE, rounded_outside)])
            came = swap_z(send, k)
            turns.append(came)
            total = total + came[: 2 * img_tok].astype(F32)
            if last:
                gate_total = gate_total + decoded(came[2 * img_tok :])
        return total, gate_total, turns

    near_z = []
    owns = [own_columns(c) for c in range(chunks)]
    starts = [square_of(own) if c else column_of(own) for c, own in enumerate(owns)]
    sizes = (n, *block_mask.shape, heads, local_kv, queries.shape[0])
    plan, starts, gate_value = lax.optimization_barrier((plan, starts, gate_value))
    column = starts[0]
    gathered = [[column, swap(column, 1), swap(column, 2), swap(column, 3)]]
    shared = tuple(prepare(sizes, img_tok, plan, queries, cotangent, gathered[0][1]))
    for square in starts[1:]:
        far = [swap_z(square, k) for k in range(2, n)]
        gathered[0][1], near = lax.optimization_barrier((gathered[0][1], square))
        gathered.append([square, swap_z(near, 1)] + far)
    gate_part = jnp.zeros((8, HD), F32)
    parts, dq = [], None
    saved, waiting = [], None
    for c in range(chunks):
        last = c == chunks - 1
        outs = attention(c, sizes, gate_value, gate_part, gathered[c], shared)
        ds, k_read, own, *backs, gate_part = outs
        if c:
            held = lax.optimization_barrier((tuple(backs), waiting[1]))
            backs = held[0]
            total, gate_row, turns = column_sum(*square_sum(waiting[0], held[1]), False)
            parts.append(total.astype(BF16))
        came = [swap(back, a + 1) for a, back in enumerate(backs)]
        waiting = (own, tuple(came))
        saved.append((ds, k_read))
    for c, (ds, k_read) in enumerate(saved):
        after = came[FIRST] if c == chunks - 1 else turns[0]
        dq = query_gradient(c, sizes, queries.shape, dq, [after], gate_value, ds, k_read)
    *came, dq = lax.optimization_barrier((*came, dq))
    total, gate_row, turns = column_sum(*square_sum(own, came), True)
    parts.append(total.astype(BF16))
    grads = jnp.concatenate(parts, axis=1)
    key_grad, value_grad = grads[None, :img_tok], grads[None, img_tok:]
    gate_total = gate_row
    for k in range(1, n_tp):
        pairs = [(i, (i + k) % n_tp) for i in range(n_tp)]
        gate_total = gate_total + lax.ppermute(gate_row, "tp", pairs)
    term_count = queries.shape[0] * n_ctx * queries.shape[1] * n_tp
    gate_row = gate_total[0, :HD] * (1.0 / math.sqrt(term_count))
    gate_grad = ((1.0 - gate_value * gate_value) * gate_row)[:1]
    return (dq, key_grad, value_grad, gate_grad)


def solution(mesh):
    in_specs = (
        P("ctx", "tp"),
        P("ctx", "tp"),
        P("ctx", None, "tp"),
        P("ctx", None, "tp"),
        P(),
        P("ctx", None),
        P(),
    )
    out_specs = (P("ctx", "tp"), P("ctx", None, "tp"), P("ctx", None, "tp"), P())
    return jax.shard_map(
        per_device, mesh=mesh, in_specs=in_specs, out_specs=out_specs, check_vma=False
    )
```
